512 devices in a mesh: tm: 512 (over x, y, z, core).
Axes of the slice: x: 4, y: 8, z: 8, core: 2. Of those that a mesh axis runs over, the one named last changes fastest.
Arguments:
- features: bfloat16 [65536, 768], P('tm'), may hold values from -256 to 256
- qkv_flat: bfloat16 [13824, 128], P('tm'), may hold values from -0.21875 to 0.21875
- out_flat: bfloat16 [4608, 128], P('tm'), may hold values from -0.21875 to 0.21875
- level_slope: float32 [12], replicated, may hold values from 0.85 to 1.4
Outputs:
- mixed: bfloat16 [65536, 768], P('tm')
The draws below stay inside these ranges and needn't reach their ends.
All inputs are finite; a program needn't handle non-finite values.
Results may differ from the reference program's by a relative error of at most 0.012.
Values may be sent and summed in bfloat16 or wider, within the bound.
A program may use at most 64 MiB of HBM per device.

```python
import math
import jax
import jax.numpy as jnp
from jax import lax

D = 768
HEADS = 12
HEAD_DIM = 64
BLOCK = 16
TOK_DEV = 128
TOKENS = 65536
N_TM = 512


def draw_features(key, part):
    key = jax.random.fold_in(key, 11)
    octaves = TOKENS.bit_length() - 1
    layered = jnp.zeros((1, D), jnp.float32)
    for octave in range(octaves, -1, -1):
        if octave < octaves:
            layered = jnp.repeat(layered, 2, axis=0)
        sub_key = jax.random.fold_in(key, octave)
        shape_now = (TOKENS >> octave, D)
        jitter = jnp.clip(jax.random.normal(sub_key, shape_now, jnp.float32), -4.0, 4.0)
        weight_now = 1.0 if octave == 0 else 0.3
        layered = layered + weight_now * jitter
    return layered.astype(jnp.bfloat16)


def steps_of(rng, extent, split, low, largest):
    def one(dim, shards_of):
        steps = jax.random.uniform(jax.random.fold_in(jax.random.fold_in(rng, 6), dim), (shards_of,), jnp.float32, low / len(split), largest / len(split))
        return jnp.repeat(jnp.exp(steps), extent[dim] // shards_of).reshape((-1,) + (1,) * (len(extent) - dim - 1))

    level = one(*split[0])
    for cut in split[1:]:
        level = level * one(*cut)
    return level


def scatter_about(key, extent, spread, reach, pieces=(), held_as=jnp.bfloat16):
    level = steps_of(key, extent, pieces, -0.22, 0.18) if pieces else 1.0
    entries = jax.random.normal(key, extent, jnp.float32) * spread * level
    return jnp.minimum(jnp.maximum(entries, -reach), reach).astype(held_as)


def setup_inputs(seed: int = 0) -> dict:
    seeds = jax.random.split(jax.random.key(seed), 5)
    return {
        "features": draw_features(jax.random.fold_in(seeds[4], 71), 0),
        "qkv_flat": scatter_about(seeds[1], (3 * D * D // 128, 128), D ** -0.5, 0.21875, ((0, 512),)),
        "out_flat": scatter_about(seeds[2], (D * D // 128, 128), D ** -0.5, 0.21875, ((0, 512),)),
        "level_slope": jnp.clip(jax.random.uniform(seeds[3], (HEADS,), jnp.float32, 0.85, 1.4), 0.85, 1.4),
    }


score_scale = 0.125
log_two = math.log(2.0)


def pair_mean(block):
    halves = block.reshape(block.shape[0] // 2, 2, block.shape[1])
    return (halves[:, 0] + halves[:, 1]) * 0.5


def pair_stats(queries, key_rows, val_rows, at_level, slope):
    row_count = queries.shape[0]
    groups = row_count // (2 * BLOCK)
    block_shape = (groups, 2, BLOCK, HEADS, HEAD_DIM)
    q_blocks = queries.astype(jnp.float32).reshape(block_shape)
    k_blocks = key_rows.astype(jnp.float32).reshape(block_shape)
    v_blocks = val_rows.astype(jnp.float32).reshape(block_shape)
    if at_level == 0:
        key_pair = k_blocks.reshape(groups, 2 * BLOCK, HEADS, HEAD_DIM)
        val_pair = v_blocks.reshape(groups, 2 * BLOCK, HEADS, HEAD_DIM)
        scores = jnp.einsum("gpihd,gjhd->gpihj", q_blocks, key_pair, precision=lax.Precision.HIGHEST) * score_scale
        maxima = jnp.max(scores, axis=-1)
        powers = jnp.exp(scores - maxima[..., None])
        rounded = lax.optimization_barrier(powers.astype(jnp.bfloat16)).astype(jnp.float32)
        numerator = jnp.einsum("gpihj,gjhd->gpihd", rounded, val_pair, precision=lax.Precision.HIGHEST)
    else:
        level_bias = at_level * log_two * (1.0 - slope)
        scores = jnp.einsum("gpihd,gpjhd->gpihj", q_blocks, k_blocks[:, ::-1], precision=lax.Precision.HIGHEST) * score_scale + level_bias[:, None]
        maxima = jnp.max(scores, axis=-1)
        powers = jnp.exp(scores - maxima[..., None])
        numerator = jnp.einsum("gpihj,gpjhd->gpihd", powers, v_blocks[:, ::-1], precision=lax.Precision.HIGHEST)
    denominator = jnp.sum(powers, axis=-1)
    return (maxima.reshape(row_count, HEADS), numerator.reshape(row_count, HEADS, HEAD_DIM), denominator.reshape(row_count, HEADS))


def combine(state, stats, factor):
    old_top, old_num, old_den = state
    new_top, new_num, new_den = [jnp.repeat(member, factor, axis=0) for member in stats]
    highest = jnp.maximum(old_top, new_top)
    old_scale = jnp.exp(old_top - highest)
    new_scale = jnp.exp(new_top - highest)
    return (highest, old_num * old_scale[..., None] + new_num * new_scale[..., None], old_den * old_scale + new_den * new_scale)


def local_levels(projected, slope):
    row_count = projected.shape[0]
    queries = projected[:, :D]
    key_rows = projected[:, D:2 * D]
    val_rows = projected[:, 2 * D:]
    state = pair_stats(queries, key_rows, val_rows, 0, slope)
    coarse = (queries.astype(jnp.float32), key_rows.astype(jnp.float32), val_rows.astype(jnp.float32))
    at_level = 1
    while (BLOCK << at_level) <= row_count:
        coarse = tuple(pair_mean(member) for member in coarse)
        if (BLOCK << (at_level + 1)) <= row_count:
            state = combine(state, pair_stats(coarse[0], coarse[1], coarse[2], at_level, slope), 1 << at_level)
        at_level += 1
    return state, coarse


def reference(features, qkv_flat, out_flat, level_slope):
    w_qkv = qkv_flat.reshape(D, 3 * D)
    w_out = out_flat.reshape(D, D)
    segments = features.reshape(N_TM, TOK_DEV, D)
    base_level = (TOK_DEV // BLOCK).bit_length() - 1
    bit_count = N_TM.bit_length() - 1

    def first_pass(segment):
        projected = jnp.dot(segment, w_qkv, preferred_element_type=jnp.float32).astype(jnp.bfloat16)
        coarse = (projected[:, :D].astype(jnp.float32), projected[:, D:2 * D].astype(jnp.float32), projected[:, 2 * D:].astype(jnp.float32))
        for level_no in range(base_level):
            coarse = tuple(pair_mean(member) for member in coarse)
        return projected, coarse

    projected_all, coarse_all = lax.map(first_pass, segments)
    coarse = tuple(member.reshape(N_TM * BLOCK, D) for member in coarse_all)
    cross = []
    for bit_no in range(bit_count):
        if bit_no > 0:
            coarse = tuple(pair_mean(member) for member in coarse)
        cross.append(pair_stats(coarse[0], coarse[1], coarse[2], base_level + bit_no, level_slope))

    def second_pass(inputs):
        projected, seg_no = inputs
        state, unused = local_levels(projected, level_slope)
        for bit_no in range(bit_count):
            row_span = max(BLOCK >> bit_no, 1)
            row_start = (seg_no * BLOCK) // (1 << bit_no)
            piece = tuple(lax.dynamic_slice_in_dim(member, row_start, row_span, 0) for member in cross[bit_no])
            state = combine(state, piece, TOK_DEV // row_span)
        highest, numerator, denominator = state
        attended = (numerator / denominator[..., None]).reshape(TOK_DEV, D).astype(jnp.bfloat16)
        return jnp.dot(attended, w_out, preferred_element_type=jnp.float32).astype(jnp.bfloat16)

    mixed = lax.map(second_pass, (projected_all, jnp.arange(N_TM, dtype=jnp.int32)))
    return mixed.reshape(N_TM * TOK_DEV, D)
```

```python
import math

import jax
import jax.numpy as jnp
from jax import lax
from jax.experimental import pallas as pl
from jax.experimental.pallas import tpu as pltpu
from jax.sharding import PartitionSpec as P

D = 768
HEADS = 12
HEAD_DIM = 64
BLOCK = 16
TOK = 128
NX, NY, NZ = 4, 8, 8
NG = NY // 2
SEL = 12
SEL_A = 8
RAW = 48
KROWS = 48
LOG_TWO = math.log(2.0)
F32, BF16, I32 = jnp.float32, jnp.bfloat16, jnp.int32
MESH = pl.DeviceIdType.MESH


def iota(shape, dim):
    return lax.broadcasted_iota(I32, shape, dim)


def pick(condition, value=1.0):
    return jnp.where(condition, value, 0.0).astype(BF16)


def mm(a, b):
    return jnp.dot(a, b, preferred_element_type=F32)


def mm_nt(a, b):
    return lax.dot_general(a, b, (((1,), (1,)), ((), ())), preferred_element_type=F32)


def third(value):
    return lax.shift_right_logical(value * 171, 9)


def line_rows(place):
    row, col = iota((64, 128), 0), iota((64, 128), 1)
    r = row & 15
    first = pick((row < 16) & (col == 16 * (place ^ 1) + r))
    second = pick((row >= 16) & (row < 32) & ((col >> 1) == 16 * ((place >> 1) ^ 1) + r), 0.5)
    fourth = pick((row >= 32) & (row < 48) & ((col >> 2) == 16 * ((place >> 2) ^ 1) + r), 0.25)
    whole = pick((row >= 48) & ((col >> 3) == r), 0.125)
    return first + second + fourth + whole


def body(
    x_ref, qkv_ref, out_ref, slope_ref, o_ref,
    raw, stage, gather, buf_a, buf_b, feat3, feat4, feat7, feat10,
    rows, perm, expand, q_all, k_all, v_all, q_exp, attended,
    send, recv,
):
    me = lax.axis_index("tm")
    x, y, z, c = me // 128, (me // 16) % 8, (me // 2) % 8, me % 2
    yg, yp = y // 2, y % 2

    def at(px, py, pz, pc):
        return ((px * NY + py) * NZ + pz) * 2 + pc

    sibling = at(x, y, z, 1 - c)
    z_line = [at(x, y, (z + j) % 8, c) for j in range(1, 8)]
    z_other = [at(x, y + 1 - 2 * yp, (z + j) % 8, c) for j in range(8)]
    y_line = [at(x, (y + j) % 8, z, c) for j in range(1, 8)]
    y_even = [at(x, (y + 2 * j) % 8, z, c) for j in range(1, 4)]
    x_line = [at((x + j) % 4, y, z, c) for j in range(1, 4)]

    barrier = pltpu.get_barrier_semaphore()
    greet = [sibling] + z_line + z_other + y_line + x_line
    for other in greet:
        pl.semaphore_signal(barrier, inc=1, device_id=(other,), device_id_type=MESH)

    count = [0]

    def copy(src, dst, device):
        slot = count[0]
        count[0] += 1
        made = pltpu.make_async_remote_copy(
            src_ref=src, dst_ref=dst, send_sem=send.at[slot], recv_sem=recv.at[slot],
            device_id=(device,), device_id_type=MESH,
        )
        made.start()
        sent.append(made)
        return made

    sent = []

    stage[...] = jnp.zeros((RAW, 128), F32)
    stage[0:27, :] = qkv_ref[...].astype(F32)
    stage[32:41, :] = out_ref[...].astype(F32)
    raw[c] = stage[...].astype(BF16)
    tokens = x_ref[...]
    rows[0:128, :] = tokens
    row, col = iota((16, 128), 0), iota((16, 128), 1)
    feat3[c] = mm(pick((col >> 3) == row, 0.125), tokens).astype(BF16)
    row, col = iota((RAW, 2 * RAW), 0), iota((RAW, 2 * RAW), 1)
    k = third(row) >> 2
    rest = row - 12 * k
    s = third(rest)
    j = rest - 3 * s
    flat = jnp.where(s < 3, k * 18 + s * 6, k * 6) + 3 * c + j
    half = jnp.where(s < 3, 27, 9)
    side = (flat >= half).astype(I32)
    source = side * RAW + flat - half * side + jnp.where(s < 3, 0, 32)
    choose = pick((row < 36) & (col == source))
    row, col = iota((SEL * KROWS, 16 * RAW), 0), iota((SEL * KROWS, 16 * RAW), 1)
    n = third(row >> 4)
    rest = row - 48 * n
    i = third(rest)
    k = rest - 3 * i
    perm[...] = pick(col == i * 48 + k * 12 + n)
    for level in range(1, 12):
        row, col = iota((128, 144), 0), iota((128, 144), 1)
        if level < 8:
            hit = (col < 128) & ((col >> level) == (row >> level))
            expand[pl.ds((level - 1) * 128, 128), :] = pick(hit, 0.125 / (1 << level))
        else:
            expand[pl.ds((level - 1) * 128, 128), :] = pick(col == 128 + level - 8, 0.125)

    pl.semaphore_wait(barrier, len(greet))

    a = copy(raw.at[c], raw.at[c], sibling)
    b = copy(feat3.at[c], feat3.at[c], sibling)
    a.wait_recv()
    spot = yp * 8 + z
    gather[spot] = mm(choose, raw[...].reshape(2 * RAW, 128)).astype(BF16)
    first = [copy(gather.at[spot], gather.at[spot], other) for other in z_line + z_other]
    b.wait_recv()
    row, col = iota((16, 32), 0), iota((16, 32), 1)
    feat4[z] = mm(pick((col >> 1) == row, 0.5), feat3[...].reshape(32, D)).astype(BF16)
    line = [copy(feat4.at[z], feat4.at[z], other) for other in z_line]
    rows[144:160, :] = feat3[1 - c]

    for made in first:
        made.wait_recv()
    chunk = mm(perm[...], gather[...].reshape(16 * RAW, 128)).astype(BF16)
    buf_a[c, x, yg] = chunk[: SEL_A * KROWS]
    buf_b[c, yg, x] = chunk[SEL_A * KROWS :]
    a2 = [copy(buf_a.at[c, x, yg], buf_a.at[c, x, yg], other) for other in y_even]
    b2 = [copy(buf_b.at[c, yg, x], buf_b.at[c, yg, x], other) for other in x_line]

    for made in line:
        made.wait_recv()
    z_rows = feat4[...].reshape(128, D)
    found = mm(line_rows(z), z_rows).astype(BF16)
    rows[160:208, :] = found[:48]
    feat7[y] = found[48:]
    line = [copy(feat7.at[y], feat7.at[y], other) for other in y_line]
    row, col = iota((16, 128), 0), iota((16, 128), 1)
    span = row + 4
    means = (
        pick((row == 0) & ((col >> 4) == z), 1 / 16)
        + pick((row == 1) & ((col >> 5) == (z >> 1)), 1 / 32)
        + pick((row == 2) & ((col >> 6) == (z >> 2)), 1 / 64)
        + pick(row == 3, 1 / 128)
    )
    rows[128:144, :] = mm(means, z_rows).astype(BF16)

    for made in a2:
        made.wait_recv()
    a3 = [copy(buf_a.at[c, x], buf_a.at[c, x], other) for other in x_line]
    across = [copy(buf_a.at[c, x], buf_a.at[c, x], sibling)]
    for made in b2:
        made.wait_recv()
    b3 = [copy(buf_b.at[c, yg], buf_b.at[c, yg], other) for other in y_even]
    across.append(copy(buf_b.at[c, yg], buf_b.at[c, yg], sibling))

    for made in line:
        made.wait_recv()
    found = mm(line_rows(y), feat7[...].reshape(128, D)).astype(BF16)
    rows[208:256, :] = found[:48]
    feat10[x] = found[48:]
    line = [copy(feat10.at[x], feat10.at[x], other) for other in x_line]
    for made in line:
        made.wait_recv()
    row, col = iota((32, 64), 0), iota((32, 64), 1)
    sides = pick((row < 16) & (col == 16 * (x ^ 1) + row)) + pick(
        (row >= 16) & ((col >> 1) == 16 * ((x >> 1) ^ 1) + row - 16), 0.5
    )
    rows[256:288, :] = mm(sides, feat10[...].reshape(64, D)).astype(BF16)

    for j, made in enumerate(a3):
        made.wait_recv()
        src = buf_a.at[c, (x + 3 - j) % 4]
        across.append(copy(src, src, sibling))
    for j, made in enumerate(b3):
        made.wait_recv()
        src = buf_b.at[c, (yg + 3 - j) % 4]
        across.append(copy(src, src, sibling))
    for made in across:
        made.wait_recv()

    def weight(kind, owner, j):
        place = kind * 3 + j
        parts = []
        for px in range(NX):
            for pg in range(NG):
                if place < SEL_A:
                    parts.append(buf_a[owner, px, pg, place * KROWS : (place + 1) * KROWS, :])
                else:
                    low = place - SEL_A
                    parts.append(buf_b[owner, pg, px, low * KROWS : (low + 1) * KROWS, :])
        return jnp.concatenate(parts, axis=0)

    def weights(kind, pair):
        blocks = [weight(kind, n // 3, n % 3) for n in (2 * pair, 2 * pair + 1)]
        return jnp.concatenate(blocks, axis=1)

    row, col = iota((96, 128), 0), iota((96, 128), 1)
    pool = pick((row < 64) & ((col >> 1) == row), 0.5) + pick(
        (row >= 64) & ((col >> 2) == row - 64), 0.25
    )
    for pair in range(3):
        lanes = slice(pair * 256, (pair + 1) * 256)
        q_all[:, lanes] = mm(rows[0:144, :], weights(0, pair)).astype(BF16)
        for kind, target in ((1, k_all), (2, v_all)):
            made = mm(rows[...], weights(kind, pair)).astype(BF16)
            target[0:128, lanes] = made[0:128]
            target[128:224, lanes] = mm(pool, made[0:128]).astype(BF16)
            target[224:368, lanes] = made[144:288]
            target[368:384, lanes] = jnp.zeros((16, 256), BF16)
        q_exp[:, lanes] = mm(expand[...], q_all[:, lanes]).astype(BF16)

    eye = pick(iota((128, 128), 0) == iota((128, 128), 1))
    lane = iota((128, 128), 1)
    key = iota((128, 128), 0)
    seen0 = (key >> 5) == (lane >> 5)
    seen1 = (key[:64] >> 4) == ((lane[:64] >> 5) ^ 1)
    seen2 = (key[:32] >> 4) == ((lane[:32] >> 6) ^ 1)
    starts = [0, 128, 192] + [224 + 16 * n for n in range(9)] + [368]
    for pair in range(6):
        lanes = slice(pair * 128, (pair + 1) * 128)
        keys = k_all[:, lanes]
        head_lane = iota((384, 128), 1)
        keys0 = jnp.where(head_lane < 64, keys, jnp.zeros_like(keys))
        keys1 = jnp.where(head_lane < 64, jnp.zeros_like(keys), keys)
        values = mm_nt(eye, v_all[:, lanes]).astype(BF16)
        scores = [[], []]
        for level in range(12):
            low, high = starts[level], starts[level + 1]
            if level == 0:
                q = q_all[0:128, lanes] * jnp.asarray(0.125, BF16)
            else:
                q = q_exp[pl.ds((level - 1) * 128, 128), lanes]
            both = mm_nt(jnp.concatenate([keys0[low:high], keys1[low:high]], axis=0), q)
            for side in range(2):
                part = both[side * (high - low) : (side + 1) * (high - low)]
                if level:
                    part = part + level * LOG_TWO * (1.0 - slope_ref[2 * pair + side])
                if level < 3:
                    part = jnp.where((seen0, seen1, seen2)[level], part, -jnp.inf)
                scores[side].append(part)
        for side in range(2):
            flat = jnp.concatenate(scores[side], axis=0)
            top = jnp.max(flat, axis=0, keepdims=True)
            powers = jnp.exp(flat - top)
            total = jnp.sum(powers, axis=0, keepdims=True)
            powers = jnp.concatenate([powers, jnp.zeros((16, 128), F32)], axis=0).astype(BF16)
            part = mm(values[side * 64 : (side + 1) * 64], powers)
            attended[pl.ds(pair * 128 + side * 64, 64), :] = (part / total).astype(BF16)
    ready = mm_nt(eye, attended[...]).astype(BF16)
    for pair in range(3):
        o_ref[:, pair * 256 : (pair + 1) * 256] = mm(ready, weights(3, pair)).astype(BF16)

    for made in sent:
        made.wait_send()


COPIES = 80


def shards(features, qkv_flat, out_flat, level_slope):
    vmem = pl.BlockSpec(memory_space=pltpu.VMEM)
    return pl.pallas_call(
        body,
        out_shape=jax.ShapeDtypeStruct((TOK, D), BF16),
        in_specs=[vmem, vmem, vmem, pl.BlockSpec(memory_space=pltpu.SMEM)],
        out_specs=vmem,
        scratch_shapes=[
            pltpu.VMEM((2, RAW, 128), BF16),
            pltpu.VMEM((RAW, 128), F32),
            pltpu.VMEM((16, RAW, 128), BF16),
            pltpu.VMEM((2, NX, NG, SEL_A * KROWS, 128), BF16),
            pltpu.VMEM((2, NG, NX, (SEL - SEL_A) * KROWS, 128), BF16),
            pltpu.VMEM((2, 16, D), BF16),
            pltpu.VMEM((NZ, 16, D), BF16),
            pltpu.VMEM((NY, 16, D), BF16),
            pltpu.VMEM((NX, 16, D), BF16),
            pltpu.VMEM((288, D), BF16),
            pltpu.VMEM((SEL * KROWS, 16 * RAW), BF16),
            pltpu.VMEM((11 * 128, 144), BF16),
            pltpu.VMEM((144, D), BF16),
            pltpu.VMEM((384, D), BF16),
            pltpu.VMEM((384, D), BF16),
            pltpu.VMEM((11 * 128, D), BF16),
            pltpu.VMEM((D, 128), BF16),
            pltpu.SemaphoreType.DMA((COPIES,)),
            pltpu.SemaphoreType.DMA((COPIES,)),
        ],
        compiler_params=pltpu.CompilerParams(
            collective_id=0, has_side_effects=True, vmem_limit_bytes=48 * 2**20
        ),
        name="layer",
    )(features, qkv_flat, out_flat, level_slope)


def solution(mesh):
    in_specs = (P("tm", None), P("tm", None), P("tm", None), P())
    return jax.shard_map(
        shards, mesh=mesh, in_specs=in_specs, out_specs=P("tm", None), check_vma=False
    )
```

```python
import math

import jax
import jax.numpy as jnp
from jax import lax
from jax.experimental import pallas as pl
from jax.experimental.pallas import tpu as pltpu
from jax.sharding import PartitionSpec as P

D = 768
HEADS = 12
HEAD_DIM = 64
BLOCK = 16
TOK = 128
NX, NY, NZ = 4, 8, 8
NG = 4
ROWS_Q, ROWS_O = 27, 9
SLOTS = 15
CUT_Q, CUT_O = 128, 80
HALF = D // 2
VMEM_BYTES = 60 * 2**20
LOG_TWO = math.log(2.0)
F32, BF16, I32 = jnp.float32, jnp.bfloat16, jnp.int32
MESH = pl.DeviceIdType.MESH


def iota(shape, dim):
    return lax.broadcasted_iota(I32, shape, dim)


def pick(condition, value=1.0):
    return jnp.where(condition, value, 0.0).astype(BF16)


def mm(a, b):
    return jnp.dot(a, b, preferred_element_type=F32)


def mm_nt(a, b):
    return lax.dot_general(a, b, (((1,), (1,)), ((), ())), preferred_element_type=F32)


def third(value):
    return lax.shift_right_logical(value * 171, 9)


def line_rows(place):
    row, col = iota((64, 128), 0), iota((64, 128), 1)
    r = row & 15
    first = pick((row < 16) & (col == 16 * (place ^ 1) + r))
    second = pick((row >= 16) & (row < 32) & ((col >> 1) == 16 * ((place >> 1) ^ 1) + r), 0.5)
    fourth = pick((row >= 32) & (row < 48) & ((col >> 2) == 16 * ((place >> 2) ^ 1) + r), 0.25)
    whole = pick((row >= 48) & ((col >> 3) == r), 0.125)
    return first + second + fourth + whole


def body(
    x_hbm, qkv_hbm, out_hbm, slope_hbm, o_ref,
    tokens_ref, qkv_ref, out_ref, slope_ref, stage, message, gather_q, gather_o, w_q, w_o,
    feat3, feat4, feat7, feat10,
    rows, order, perm, expand, q_all, k_all, v_all, q_exp, attended, away,
    send, recv, local,
):
    me = lax.axis_index("tm")
    x, y, z, c = me // 128, (me // 16) % 8, (me // 2) % 8, me % 2
    yq, yr, zq, zr = y // 4, y % 4, z // 4, z % 4

    loads = [
        pltpu.make_async_copy(x_hbm, tokens_ref, local.at[0]),
        pltpu.make_async_copy(qkv_hbm, qkv_ref, local.at[1]),
        pltpu.make_async_copy(out_hbm, out_ref, local.at[2]),
        pltpu.make_async_copy(slope_hbm, slope_ref, local.at[3]),
    ]
    for load in loads:
        load.start()

    def at(px, py, pz, pc):
        return ((px * NY + py) * NZ + pz) * 2 + pc

    sibling = at(x, y, z, 1 - c)
    steps = [(2, 2), (2, 1), (1, 2), (2, 3), (3, 2), (1, 1), (1, 3), (3, 1), (3, 3)]
    steps += [(0, 2), (2, 0), (0, 1), (1, 0), (0, 3), (3, 0)]
    square = [at(x, yq * 4 + (yr + j) % 4, zq * 4 + (zr + k) % 4, c) for j, k in steps]
    z_line = [at(x, y, (z + j) % 8, c) for j in (4, 3, 5, 2, 6, 1, 7)]
    y_line = [at(x, (y + j) % 8, z, c) for j in (4, 3, 5, 2, 6, 1, 7)]
    z_rest = [at(x, y, (1 - zq) * 4 + (zr + j) % 4, c) for j in range(4)]
    y_rest = [at(x, (1 - yq) * 4 + (yr + j) % 4, z, c) for j in range(4)]
    x_line = [at((x + j) % 4, y, z, c) for j in (2, 1, 3)]
    opposite, right, left = x_line
    z_mate = at(x, y, (z + 4 * (zr // 2) + 6) % 8, c)
    y_mate = at(x, (y + 4 * (yr // 2) + 6) % 8, z, c)

    barrier = pltpu.get_barrier_semaphore()
    greet = square + z_rest + y_rest + x_line + [sibling]
    for other in greet:
        pl.semaphore_signal(barrier, inc=1, device_id=(other,), device_id_type=MESH)

    sent = []

    def copy(ref, device, target=None):
        slot = len(sent)
        made = pltpu.make_async_remote_copy(
            src_ref=ref, dst_ref=ref if target is None else target, send_sem=send.at[slot], recv_sem=recv.at[slot],
            device_id=(device,), device_id_type=MESH,
        )
        made.start()
        sent.append(made)
        return made

    for load in loads:
        load.wait()
    spot = yr * 4 + zr
    heads = z % 2
    partner = at(x, y, z + 1 - 2 * heads, c)
    stage[...] = jnp.zeros((48, 128), F32)
    stage[0:ROWS_Q, :] = qkv_ref[...].astype(F32)
    stage[32 : 32 + ROWS_O, :] = out_ref[...].astype(F32)
    row, col = iota((32, 32), 0), iota((32, 32), 1)
    half, slot = row >> 4, row & 15
    s = third(slot)
    j = slot - 3 * s
    whole = 9 * c + 6 * s + 3 * half + j
    shared = jnp.where(slot < 12, 18 - 15 * c + 3 * half + j, 24 - 24 * c + j)
    source = jnp.where(slot < 9, whole, shared)
    wanted = (slot < 12) | ((slot < SLOTS) & (half == c))
    message[...] = mm(pick(wanted & (col == source)), stage[0:32, :].astype(BF16)).astype(BF16).reshape(2, 16, 128)
    gather_q[spot] = message[heads]
    gather_o[spot] = stage[32:48, :].astype(BF16)

    pl.semaphore_wait(barrier, len(greet))

    first = [
        copy(message.at[(heads + k) % 2], other, gather_q.at[spot])
        for (j, k), other in zip(steps, square)
    ]

    col = iota((1, D), 1)
    part = third(col >> 4)
    rest = col - 48 * part
    natural = (part >> 2) * 192 + ((part >> 1) & 1) * 96 + (part & 1) * 12
    natural = natural + ((rest >> 2) & 3) * 24 + (rest & 3) * 3 + (rest >> 4)
    order[...] = pick(iota((D, D), 0) == natural)
    tokens = mm(tokens_ref[...], order[...]).astype(BF16)
    rows[0:128, :] = tokens
    row, col = iota((16, 128), 0), iota((16, 128), 1)
    feat3[c] = mm(pick((col >> 3) == row, 0.125), tokens).astype(BF16)
    b = copy(feat3.at[c], sibling)
    row, col = iota((16 * SLOTS, 16 * 16), 0), iota((16 * SLOTS, 16 * 16), 1)
    perm[...] = pick(col == (row & 15) * 16 + (row >> 4))
    for level in range(1, 12):
        row, col = iota((128, 144), 0), iota((128, 144), 1)
        if level < 8:
            hit = (col < 128) & ((col >> level) == (row >> level))
            expand[pl.ds((level - 1) * 128, 128), :] = pick(hit, 0.125 / (1 << level))
        else:
            expand[pl.ds((level - 1) * 128, 128), :] = pick(col == 128 + level - 8, 0.125)

    b.wait_recv()
    mine = pl.ds(pl.multiple_of(c * HALF, 128), HALF)
    row, col = iota((16, 32), 0), iota((16, 32), 1)
    feat4[z] = mm(pick((col >> 1) == row, 0.5), feat3[:, :, mine].reshape(32, HALF)).astype(BF16)
    line = [copy(feat4.at[z], other) for other in z_line]
    second = [copy(gather_o.at[spot], other) for other in square]
    rows[432:448, :] = feat3[1 - c]
    pair3 = copy(feat3.at[1 - c], partner, rows.at[pl.ds(448, 16)])

    for made in first:
        made.wait_recv()
    own = 2 * yq + zq
    w_q[c, x, own] = mm(perm[...], gather_q[...].reshape(16 * 16, 128)).astype(BF16)
    over_z, over_y, far = 2 * yq + 1 - zq, 2 - 2 * yq + zq, 3 - own

    def got(made):
        for one in made:
            one.wait_recv()

    def along(ref):
        return [copy(ref.at[c, x, own], z_mate), copy(ref.at[c, x, own], y_mate)]

    def corner(ref, cut, size):
        return [
            copy(ref.at[c, x, over_z, pl.ds(0, cut)], y_mate),
            copy(ref.at[c, x, over_y, pl.ds(cut, size - cut)], z_mate),
        ]

    def along_x(ref, group, others):
        return [copy(ref.at[c, x, group], other) for other in others]

    def hand_on(ref, group, cut, size):
        return [
            copy(ref.at[c, (x + 3) % 4, group, pl.ds(0, cut)], right),
            copy(ref.at[c, (x + 1) % 4, group, pl.ds(cut, size - cut)], left),
        ]

    def across(ref, px, group):
        return copy(ref.at[c, px, group], sibling)

    yz_q = along(w_q)
    x_q = [along_x(w_q, own, (right, left))]

    got(line)
    z_rows = feat4[...].reshape(128, HALF)
    found = mm(line_rows(z), z_rows).astype(BF16)
    rows[400:416, mine] = found[0:16]
    rows[416:432, mine] = feat4[z]
    rows[288:320, mine] = found[16:48]
    feat7[y] = found[48:]
    line = [copy(feat7.at[y], other) for other in y_line]
    row, col = iota((32, 128), 0), iota((32, 128), 1)
    chip = jnp.where(row < 16, z, z ^ 1)
    row = row & 15
    means = (
        pick((row == 0) & ((col >> 4) == chip), 1 / 16)
        + pick((row == 1) & ((col >> 5) == (z >> 1)), 1 / 32)
        + pick((row == 2) & ((col >> 6) == (z >> 2)), 1 / 64)
        + pick(row == 3, 1 / 128)
    )
    rows[256:288, mine] = mm(means, z_rows).astype(BF16)

    yz_q[0].wait_recv()
    yz_q[1].wait_recv()
    corner_q = corner(w_q, CUT_Q, 16 * SLOTS)
    pair_tokens = copy(rows.at[pl.ds(0, 128)], partner, rows.at[pl.ds(128, 128)])
    x_q.append(along_x(w_q, over_z, (right, left)))
    x_q.append(along_x(w_q, over_y, (right, left)))
    got(x_q[0])
    relay_q = [hand_on(w_q, own, CUT_Q, 16 * SLOTS)]
    over = [across(w_q, (x + 3) % 4, own), across(w_q, (x + 1) % 4, own)]
    got(second)
    w_o[c, x, own] = mm(perm[0 : 16 * ROWS_O, :], gather_o[...].reshape(16 * 16, 128)).astype(BF16)

    got(line)
    found = mm(line_rows(y), feat7[...].reshape(128, HALF)).astype(BF16)
    rows[320:368, mine] = found[:48]
    feat10[x] = found[48:]
    line = [copy(feat10.at[x], other) for other in x_line]

    got(corner_q)
    x_q.append(along_x(w_q, far, (opposite, right, left)))
    over.append(copy(w_q.at[c, x], sibling))
    yz_o = along(w_o)
    for n, group in ((1, over_z), (2, over_y)):
        got(x_q[n])
        relay_q.append(hand_on(w_q, group, CUT_Q, 16 * SLOTS))
        over += [across(w_q, (x + 3) % 4, group), across(w_q, (x + 1) % 4, group)]

    got(line)
    row, col = iota((32, 64), 0), iota((32, 64), 1)
    sides = pick((row < 16) & (col == 16 * (x ^ 1) + row)) + pick(
        (row >= 16) & ((col >> 1) == 16 * ((x >> 1) ^ 1) + row - 16), 0.5
    )
    rows[368:400, mine] = mm(sides, feat10[...].reshape(64, HALF)).astype(BF16)
    coarse = copy(rows.at[pl.ds(256, 176), mine], sibling)

    for made, group in zip(relay_q, (own, over_z, over_y)):
        got(made)
        over.append(across(w_q, (x + 2) % 4, group))
    got(yz_o)
    corner_o = corner(w_o, CUT_O, 16 * ROWS_O)
    x_o = [along_x(w_o, group, x_line) for group in (own, over_z, over_y)]
    x_q[3][1].wait_recv()
    over.append(across(w_q, (x + 3) % 4, far))
    x_q[3][2].wait_recv()
    over.append(across(w_q, (x + 1) % 4, far))
    x_q[3][0].wait_recv()
    over.append(across(w_q, (x + 2) % 4, far))
    coarse.wait_recv()
    pair3.wait_recv()
    pair_tokens.wait_recv()
    got(over)

    def tiles(sources):
        parts = []
        for px in range(NX):
            for group in range(NG):
                for ref, owner, place in sources:
                    parts.append(ref[owner, px, group, place * 16 : place * 16 + 16, :])
        return jnp.concatenate(parts, axis=0)

    def weight_q(s, j):
        second = ((0, 9 + j), (heads, 12 + j), (1, 9 + j))[s]
        return tiles([(w_q, 0, 3 * s + j), (w_q, *second), (w_q, 1, 3 * s + j)])

    def weight_o(n):
        second = (0, 6 + n) if n < 3 else (1, n - 3)
        return tiles([(w_o, 0, n), (w_o, *second), (w_o, 1, 3 + n)])

    row, col = iota((96, 128), 0), iota((96, 128), 1)
    pool = pick((row < 64) & ((col >> 1) == row), 0.5) + pick(
        (row >= 64) & ((col >> 2) == row - 64), 0.25
    )
    made = mm(rows[0:288, :], jnp.concatenate([weight_q(0, j) for j in range(3)], axis=1)).astype(BF16)
    for seg in range(2):
        q_all[seg, 0:128, :] = made[128 * seg : 128 * seg + 128]
        q_all[seg, 128:144, :] = made[256 + 16 * seg : 272 + 16 * seg]
        q_exp[seg] = mm(expand[...], q_all[seg]).astype(BF16)
    for kind, target in ((1, k_all), (2, v_all)):
        made = mm(rows[...], jnp.concatenate([weight_q(kind, j) for j in range(3)], axis=1)).astype(BF16)
        for seg in range(2):
            base = made[128 * seg : 128 * seg + 128]
            target[seg, 0:128, :] = base
            target[seg, 128:224, :] = mm(pool, base).astype(BF16)
            target[seg, 224:336, :] = made[288:400]
            target[seg, 336:352, :] = made[400 + 16 * seg : 416 + 16 * seg]
            target[seg, 352:368, :] = made[432 + 16 * seg : 448 + 16 * seg]
            target[seg, 368:384, :] = jnp.zeros((16, HALF), BF16)

    got(corner_o)
    x_o.append(along_x(w_o, far, x_line))
    over = [copy(w_o.at[c, x], sibling)]

    eye = pick(iota((128, 128), 0) == iota((128, 128), 1))
    lane = iota((128, 128), 1)
    key = iota((128, 128), 0)
    seen0 = (key >> 5) == (lane >> 5)
    seen1 = (key[:64] >> 4) == ((lane[:64] >> 5) ^ 1)
    seen2 = (key[:32] >> 4) == ((lane[:32] >> 6) ^ 1)
    spans = [(0, 0, 128), (1, 128, 192), (2, 192, 224)]
    spans += [(n, 144 + 16 * n, 160 + 16 * n) for n in range(5, 12)] + [(4, 336, 352), (3, 352, 368)]
    back = []
    for seg, pair in [(1, 0), (1, 1), (1, 2), (0, 0), (0, 1), (0, 2)]:
        lanes = slice(pair * 128, (pair + 1) * 128)
        keys = k_all[seg, :, lanes]
        head_lane = iota((384, 128), 1)
        keys0 = jnp.where(head_lane < 64, keys, jnp.zeros_like(keys))
        keys1 = jnp.where(head_lane < 64, jnp.zeros_like(keys), keys)
        values = mm_nt(eye, v_all[seg, :, lanes]).astype(BF16)
        scores = [[], []]
        for level, low, high in spans:
            if level == 0:
                q = q_all[seg, 0:128, lanes] * jnp.asarray(0.125, BF16)
            else:
                q = q_exp[seg, pl.ds((level - 1) * 128, 128), lanes]
            both = mm_nt(jnp.concatenate([keys0[low:high], keys1[low:high]], axis=0), q)
            for side in range(2):
                part = both[side * (high - low) : (side + 1) * (high - low)]
                if level:
                    part = part + level * LOG_TWO * (1.0 - slope_ref[6 * heads + 2 * pair + side])
                if level < 3:
                    part = jnp.where((seen0, seen1, seen2)[level], part, -jnp.inf)
                scores[side].append(part)
        for side in range(2):
            flat = jnp.concatenate(scores[side], axis=0)
            top = jnp.max(flat, axis=0, keepdims=True)
            powers = jnp.exp(flat - top)
            total = jnp.sum(powers, axis=0, keepdims=True)
            powers = jnp.concatenate([powers, jnp.zeros((16, 128), F32)], axis=0).astype(BF16)
            part = mm(values[side * 64 : (side + 1) * 64], powers)
            part = (part / total).astype(BF16)
            if seg:
                away[pl.ds(pair * 128 + side * 64, 64), :] = part
            else:
                attended[heads, pl.ds(pair * 128 + side * 64, 64), :] = part
        if seg:
            piece = pl.ds(pair * 128, 128)
            back.append(copy(away.at[piece], partner, attended.at[heads, piece]))
    got(back)
    ready = mm(mm_nt(eye, attended[...].reshape(D, 128)).astype(BF16), order[...]).astype(BF16)

    for made in x_o:
        got(made)
    over += [copy(w_o.at[c, (x + j) % 4], sibling) for j in (1, 2, 3)]
    got(over)
    for pair in range(3):
        w = jnp.concatenate([weight_o(2 * pair), weight_o(2 * pair + 1)], axis=1)
        o_ref[:, pair * 256 : (pair + 1) * 256] = mm(ready, w).astype(BF16)

    for made in sent:
        made.wait_send()


COPIES = 128


def shards(features, qkv_flat, out_flat, level_slope):
    hbm = pl.BlockSpec(memory_space=pl.ANY)
    return pl.pallas_call(
        body,
        out_shape=jax.ShapeDtypeStruct((TOK, D), BF16),
        in_specs=[hbm] * 4,
        out_specs=pl.BlockSpec(memory_space=pltpu.VMEM),
        scratch_shapes=[
            pltpu.VMEM((TOK, D), BF16),
            pltpu.VMEM((ROWS_Q, 128), BF16),
            pltpu.VMEM((ROWS_O, 128), BF16),
            pltpu.SMEM((HEADS,), F32),
            pltpu.VMEM((48, 128), F32),
            pltpu.VMEM((2, 16, 128), BF16),
            pltpu.VMEM((16, 16, 128), BF16),
            pltpu.VMEM((16, 16, 128), BF16),
            pltpu.VMEM((2, NX, NG, 16 * SLOTS, 128), BF16),
            pltpu.VMEM((2, NX, NG, 16 * ROWS_O, 128), BF16),
            pltpu.VMEM((2, 16, D), BF16),
            pltpu.VMEM((NZ, 16, HALF), BF16),
            pltpu.VMEM((NY, 16, HALF), BF16),
            pltpu.VMEM((NX, 16, HALF), BF16),
            pltpu.VMEM((464, D), BF16),
            pltpu.VMEM((D, D), BF16),
            pltpu.VMEM((16 * SLOTS, 16 * 16), BF16),
            pltpu.VMEM((11 * 128, 144), BF16),
            pltpu.VMEM((2, 144, HALF), BF16),
            pltpu.VMEM((2, 384, HALF), BF16),
            pltpu.VMEM((2, 384, HALF), BF16),
            pltpu.VMEM((2, 11 * 128, HALF), BF16),
            pltpu.VMEM((2, HALF, 128), BF16),
            pltpu.VMEM((HALF, 128), BF16),
            pltpu.SemaphoreType.DMA((COPIES,)),
            pltpu.SemaphoreType.DMA((COPIES,)),
            pltpu.SemaphoreType.DMA((4,)),
        ],
        compiler_params=pltpu.CompilerParams(
            collective_id=0, has_side_effects=True, vmem_limit_bytes=VMEM_BYTES
        ),
        name="layer",
    )(features, qkv_flat, out_flat, level_slope)


def solution(mesh):
    in_specs = (P("tm", None), P("tm", None), P("tm", None), P())
    return jax.shard_map(
        shards, mesh=mesh, in_specs=in_specs, out_specs=P("tm", None), check_vma=False
    )
```

```python
import math

import jax
import jax.numpy as jnp
from jax import lax
from jax.experimental import pallas as pl
from jax.experimental.pallas import tpu as pltpu
from jax.sharding import PartitionSpec as P

D = 768
HEADS = 12
HEAD_DIM = 64
BLOCK = 16
TOK = 128
NX, NY, NZ = 4, 8, 8
NG = 4
ROWS_Q, ROWS_O = 27, 9
SLOTS = 15
CUT_Q, CUT_O = 128, 80
HALF = D // 2
VMEM_BYTES = 60 * 2**20
LOG_TWO = math.log(2.0)
F32, BF16, I32 = jnp.float32, jnp.bfloat16, jnp.int32
MESH = pl.DeviceIdType.MESH


def iota(shape, dim):
    return lax.broadcasted_iota(I32, shape, dim)


def pick(condition, value=1.0):
    return jnp.where(condition, value, 0.0).astype(BF16)


def mm(a, b):
    return jnp.dot(a, b, preferred_element_type=F32)


def mm_nt(a, b):
    return lax.dot_general(a, b, (((1,), (1,)), ((), ())), preferred_element_type=F32)


def third(value):
    return lax.shift_right_logical(value * 171, 9)


def line_rows(place):
    row, col = iota((64, 128), 0), iota((64, 128), 1)
    r = row & 15
    first = pick((row < 16) & (col == 16 * (place ^ 1) + r))
    second = pick((row >= 16) & (row < 32) & ((col >> 1) == 16 * ((place >> 1) ^ 1) + r), 0.5)
    fourth = pick((row >= 32) & (row < 48) & ((col >> 2) == 16 * ((place >> 2) ^ 1) + r), 0.25)
    whole = pick((row >= 48) & ((col >> 3) == r), 0.125)
    return first + second + fourth + whole


def body(
    x_hbm, qkv_hbm, out_hbm, slope_hbm, o_ref,
    tokens_ref, qkv_ref, out_ref, slope_ref, stage, message, gather_q, gather_o, w_q, w_o,
    feat3, feat4, feat7, feat10,
    rows, order, perm, expand, q_all, k_all, v_all, q_exp, attended, away,
    send, recv, local,
):
    me = lax.axis_index("tm")
    x, y, z, c = me // 128, (me // 16) % 8, (me // 2) % 8, me % 2
    yq, yr, zq, zr = y // 4, y % 4, z // 4, z % 4

    loads = [
        pltpu.make_async_copy(x_hbm, tokens_ref, local.at[0]),
        pltpu.make_async_copy(qkv_hbm, qkv_ref, local.at[1]),
        pltpu.make_async_copy(out_hbm, out_ref, local.at[2]),
        pltpu.make_async_copy(slope_hbm, slope_ref, local.at[3]),
    ]
    for load in loads:
        load.start()

    def at(px, py, pz, pc):
        return ((px * NY + py) * NZ + pz) * 2 + pc

    sibling = at(x, y, z, 1 - c)
    steps = [(2, 2), (2, 1), (1, 2), (2, 3), (3, 2), (1, 1), (1, 3), (3, 1), (3, 3)]
    steps += [(0, 2), (2, 0), (0, 1), (1, 0), (0, 3), (3, 0)]
    square = [at(x, yq * 4 + (yr + j) % 4, zq * 4 + (zr + k) % 4, c) for j, k in steps]
    z_line = [at(x, y, (z + j) % 8, c) for j in (4, 3, 5, 2, 6, 1, 7)]
    y_line = [at(x, (y + j) % 8, z, c) for j in (4, 3, 5, 2, 6, 1, 7)]
    z_rest = [at(x, y, (1 - zq) * 4 + (zr + j) % 4, c) for j in range(4)]
    y_rest = [at(x, (1 - yq) * 4 + (yr + j) % 4, z, c) for j in range(4)]
    x_line = [at((x + j) % 4, y, z, c) for j in (2, 1, 3)]
    opposite, right, left = x_line
    z_mate = at(x, y, (z + 4 * (zr // 2) + 6) % 8, c)
    y_mate = at(x, (y + 4 * (yr // 2) + 6) % 8, z, c)

    barrier = pltpu.get_barrier_semaphore()
    greet = square + z_rest + y_rest + x_line + [sibling]
    for other in greet:
        pl.semaphore_signal(barrier, inc=1, device_id=(other,), device_id_type=MESH)

    sent = []

    def copy(ref, device, target=None):
        slot = len(sent)
        made = pltpu.make_async_remote_copy(
            src_ref=ref, dst_ref=ref if target is None else target, send_sem=send.at[slot], recv_sem=recv.at[slot],
            device_id=(device,), device_id_type=MESH,
        )
        made.start()
        sent.append(made)
        return made

    for load in loads:
        load.wait()
    spot = yr * 4 + zr
    heads = z % 2
    partner = at(x, y, z + 1 - 2 * heads, c)
    stage[...] = jnp.zeros((48, 128), F32)
    stage[0:ROWS_Q, :] = qkv_ref[...].astype(F32)
    stage[32 : 32 + ROWS_O, :] = out_ref[...].astype(F32)
    row, col = iota((32, 32), 0), iota((32, 32), 1)
    half, slot = row >> 4, row & 15
    s = third(slot)
    j = slot - 3 * s
    whole = 9 * c + 6 * s + 3 * half + j
    shared = jnp.where(slot < 12, 18 - 15 * c + 3 * half + j, 24 - 24 * c + j)
    source = jnp.where(slot < 9, whole, shared)
    wanted = (slot < 12) | ((slot < SLOTS) & (half == c))
    message[...] = mm(pick(wanted & (col == source)), stage[0:32, :].astype(BF16)).astype(BF16).reshape(2, 16, 128)
    gather_q[spot] = message[heads]
    gather_o[spot] = stage[32:48, :].astype(BF16)

    pl.semaphore_wait(barrier, len(greet))

    first = [
        copy(message.at[(heads + k) % 2], other, gather_q.at[spot])
        for (j, k), other in zip(steps, square)
    ]

    col = iota((1, D), 1)
    part = third(col >> 4)
    rest = col - 48 * part
    natural = (part >> 2) * 192 + ((part >> 1) & 1) * 96 + (part & 1) * 12
    natural = natural + ((rest >> 2) & 3) * 24 + (rest & 3) * 3 + (rest >> 4)
    order[...] = pick(iota((D, D), 0) == natural)
    tokens = mm(tokens_ref[...], order[...]).astype(BF16)
    rows[0:128, :] = tokens
    row, col = iota((16, 128), 0), iota((16, 128), 1)
    feat3[c] = mm(pick((col >> 3) == row, 0.125), tokens).astype(BF16)
    b = copy(feat3.at[c], sibling)
    row, col = iota((16 * SLOTS, 16 * 16), 0), iota((16 * SLOTS, 16 * 16), 1)
    perm[...] = pick(col == (row & 15) * 16 + (row >> 4))
    for level in range(1, 12):
        row, col = iota((128, 144), 0), iota((128, 144), 1)
        if level < 8:
            hit = (col < 128) & ((col >> level) == (row >> level))
            expand[pl.ds((level - 1) * 128, 128), :] = pick(hit, 0.125 / (1 << level))
        else:
            expand[pl.ds((level - 1) * 128, 128), :] = pick(col == 128 + level - 8, 0.125)

    b.wait_recv()
    mine = pl.ds(pl.multiple_of(c * HALF, 128), HALF)
    row, col = iota((16, 32), 0), iota((16, 32), 1)
    feat4[z] = mm(pick((col >> 1) == row, 0.5), feat3[:, :, mine].reshape(32, HALF)).astype(BF16)
    line = [copy(feat4.at[z], other) for other in z_line]
    second = [copy(gather_o.at[spot], other) for other in square]
    rows[432:448, :] = feat3[1 - c]
    pair3 = copy(feat3.at[1 - c], partner, rows.at[pl.ds(448, 16)])

    for made in first:
        made.wait_recv()
    own = 2 * yq + zq
    w_q[c, x, own] = mm(perm[...], gather_q[...].reshape(16 * 16, 128)).astype(BF16)
    over_z, over_y, far = 2 * yq + 1 - zq, 2 - 2 * yq + zq, 3 - own

    def got(made):
        for one in made:
            one.wait_recv()

    def along(ref):
        return [copy(ref.at[c, x, own], z_mate), copy(ref.at[c, x, own], y_mate)]

    def corner(ref, cut, size):
        return [
            copy(ref.at[c, x, over_z, pl.ds(0, cut)], y_mate),
            copy(ref.at[c, x, over_y, pl.ds(cut, size - cut)], z_mate),
        ]

    def along_x(ref, group, others):
        return [copy(ref.at[c, x, group], other) for other in others]

    def across(ref, px, group):
        return copy(ref.at[c, px, group], sibling)

    yz_q = along(w_q)
    x_q = [along_x(w_q, own, (opposite, right, left))]

    got(line)
    z_rows = feat4[...].reshape(128, HALF)
    found = mm(line_rows(z), z_rows).astype(BF16)
    rows[400:416, mine] = found[0:16]
    rows[416:432, mine] = feat4[z]
    rows[288:320, mine] = found[16:48]
    feat7[y] = found[48:]
    line = [copy(feat7.at[y], other) for other in y_line]
    row, col = iota((32, 128), 0), iota((32, 128), 1)
    chip = jnp.where(row < 16, z, z ^ 1)
    row = row & 15
    means = (
        pick((row == 0) & ((col >> 4) == chip), 1 / 16)
        + pick((row == 1) & ((col >> 5) == (z >> 1)), 1 / 32)
        + pick((row == 2) & ((col >> 6) == (z >> 2)), 1 / 64)
        + pick(row == 3, 1 / 128)
    )
    rows[256:288, mine] = mm(means, z_rows).astype(BF16)

    yz_q[0].wait_recv()
    yz_q[1].wait_recv()
    corner_q = corner(w_q, CUT_Q, 16 * SLOTS)
    pair_tokens = copy(rows.at[pl.ds(0, 128)], partner, rows.at[pl.ds(128, 128)])
    x_q.append(along_x(w_q, over_z, (opposite, right, left)))
    x_q.append(along_x(w_q, over_y, (opposite, right, left)))
    got(x_q[0])
    over = [across(w_q, (x + j) % 4, own) for j in (1, 2, 3)]
    got(second)
    w_o[c, x, own] = mm(perm[0 : 16 * ROWS_O, :], gather_o[...].reshape(16 * 16, 128)).astype(BF16)

    got(line)
    found = mm(line_rows(y), feat7[...].reshape(128, HALF)).astype(BF16)
    rows[320:368, mine] = found[:48]
    feat10[x] = found[48:]
    line = [copy(feat10.at[x], other) for other in x_line]

    got(corner_q)
    x_q.append(along_x(w_q, far, (opposite, right, left)))
    over.append(copy(w_q.at[c, x], sibling))
    yz_o = along(w_o)
    for n, group in ((1, over_z), (2, over_y)):
        got(x_q[n])
        over += [across(w_q, (x + j) % 4, group) for j in (1, 2, 3)]

    got(line)
    row, col = iota((32, 64), 0), iota((32, 64), 1)
    sides = pick((row < 16) & (col == 16 * (x ^ 1) + row)) + pick(
        (row >= 16) & ((col >> 1) == 16 * ((x >> 1) ^ 1) + row - 16), 0.5
    )
    rows[368:400, mine] = mm(sides, feat10[...].reshape(64, HALF)).astype(BF16)
    coarse = copy(rows.at[pl.ds(256, 176), mine], sibling)

    got(yz_o)
    corner_o = corner(w_o, CUT_O, 16 * ROWS_O)
    x_q[3][1].wait_recv()
    over.append(across(w_q, (x + 3) % 4, far))
    x_q[3][2].wait_recv()
    over.append(across(w_q, (x + 1) % 4, far))
    x_q[3][0].wait_recv()
    over.append(across(w_q, (x + 2) % 4, far))
    coarse.wait_recv()
    pair3.wait_recv()
    pair_tokens.wait_recv()
    got(corner_o)
    x_o = [copy(w_o.at[c, x], other) for other in x_line]
    got(over)
    over = [copy(w_o.at[c, x], sibling)]

    def tiles(sources):
        parts = []
        for px in range(NX):
            for group in range(NG):
                for ref, owner, place in sources:
                    parts.append(ref[owner, px, group, place * 16 : place * 16 + 16, :])
        return jnp.concatenate(parts, axis=0)

    def weight_q(s, j):
        second = ((0, 9 + j), (heads, 12 + j), (1, 9 + j))[s]
        return tiles([(w_q, 0, 3 * s + j), (w_q, *second), (w_q, 1, 3 * s + j)])

    def weight_o(n):
        second = (0, 6 + n) if n < 3 else (1, n - 3)
        return tiles([(w_o, 0, n), (w_o, *second), (w_o, 1, 3 + n)])

    row, col = iota((96, 128), 0), iota((96, 128), 1)
    pool = pick((row < 64) & ((col >> 1) == row), 0.5) + pick(
        (row >= 64) & ((col >> 2) == row - 64), 0.25
    )
    made = mm(rows[0:288, :], jnp.concatenate([weight_q(0, j) for j in range(3)], axis=1)).astype(BF16)
    for seg in range(2):
        q_all[seg, 0:128, :] = made[128 * seg : 128 * seg + 128]
        q_all[seg, 128:144, :] = made[256 + 16 * seg : 272 + 16 * seg]
        q_exp[seg] = mm(expand[...], q_all[seg]).astype(BF16)
    for kind, target in ((1, k_all), (2, v_all)):
        made = mm(rows[...], jnp.concatenate([weight_q(kind, j) for j in range(3)], axis=1)).astype(BF16)
        for seg in range(2):
            base = made[128 * seg : 128 * seg + 128]
            target[seg, 0:128, :] = base
            target[seg, 128:224, :] = mm(pool, base).astype(BF16)
            target[seg, 224:336, :] = made[288:400]
            target[seg, 336:352, :] = made[400 + 16 * seg : 416 + 16 * seg]
            target[seg, 352:368, :] = made[432 + 16 * seg : 448 + 16 * seg]
            target[seg, 368:384, :] = jnp.zeros((16, HALF), BF16)

    eye = pick(iota((128, 128), 0) == iota((128, 128), 1))
    lane = iota((128, 128), 1)
    key = iota((128, 128), 0)
    seen0 = (key >> 5) == (lane >> 5)
    seen1 = (key[:64] >> 4) == ((lane[:64] >> 5) ^ 1)
    seen2 = (key[:32] >> 4) == ((lane[:32] >> 6) ^ 1)
    spans = [(0, 0, 128), (1, 128, 192), (2, 192, 224)]
    spans += [(n, 144 + 16 * n, 160 + 16 * n) for n in range(5, 12)] + [(4, 336, 352), (3, 352, 368)]
    back = []
    for seg, pair in [(1, 0), (1, 1), (1, 2), (0, 0), (0, 1), (0, 2)]:
        if (seg, pair) == (0, 1):
            got(x_o)
            over += [copy(w_o.at[c, (x + j) % 4], sibling) for j in (1, 2, 3)]
        lanes = slice(pair * 128, (pair + 1) * 128)
        keys = k_all[seg, :, lanes]
        head_lane = iota((384, 128), 1)
        keys0 = jnp.where(head_lane < 64, keys, jnp.zeros_like(keys))
        keys1 = jnp.where(head_lane < 64, jnp.zeros_like(keys), keys)
        values = mm_nt(eye, v_all[seg, :, lanes]).astype(BF16)
        scores = [[], []]
        for level, low, high in spans:
            if level == 0:
                q = q_all[seg, 0:128, lanes] * jnp.asarray(0.125, BF16)
            else:
                q = q_exp[seg, pl.ds((level - 1) * 128, 128), lanes]
            both = mm_nt(jnp.concatenate([keys0[low:high], keys1[low:high]], axis=0), q)
            for side in range(2):
                part = both[side * (high - low) : (side + 1) * (high - low)]
                if level:
                    part = part + level * LOG_TWO * (1.0 - slope_ref[6 * heads + 2 * pair + side])
                if level < 3:
                    part = jnp.where((seen0, seen1, seen2)[level], part, -jnp.inf)
                scores[side].append(part)
        for side in range(2):
            flat = jnp.concatenate(scores[side], axis=0)
            top = jnp.max(flat, axis=0, keepdims=True)
            powers = jnp.exp(flat - top)
            total = jnp.sum(powers, axis=0, keepdims=True)
            powers = jnp.concatenate([powers, jnp.zeros((16, 128), F32)], axis=0).astype(BF16)
            part = mm(values[side * 64 : (side + 1) * 64], powers)
            part = (part / total).astype(BF16)
            if seg:
                away[pl.ds(pair * 128 + side * 64, 64), :] = part
            else:
                attended[heads, pl.ds(pair * 128 + side * 64, 64), :] = part
        if seg:
            piece = pl.ds(pair * 128, 128)
            back.append(copy(away.at[piece], partner, attended.at[heads, piece]))
    got(back)
    ready = mm(mm_nt(eye, attended[...].reshape(D, 128)).astype(BF16), order[...]).astype(BF16)

    got(over)
    for pair in range(3):
        w = jnp.concatenate([weight_o(2 * pair), weight_o(2 * pair + 1)], axis=1)
        o_ref[:, pair * 256 : (pair + 1) * 256] = mm(ready, w).astype(BF16)

    for made in sent:
        made.wait_send()


COPIES = 128


def shards(features, qkv_flat, out_flat, level_slope):
    hbm = pl.BlockSpec(memory_space=pl.ANY)
    return pl.pallas_call(
        body,
        out_shape=jax.ShapeDtypeStruct((TOK, D), BF16),
        in_specs=[hbm] * 4,
        out_specs=pl.BlockSpec(memory_space=pltpu.VMEM),
        scratch_shapes=[
            pltpu.VMEM((TOK, D), BF16),
            pltpu.VMEM((ROWS_Q, 128), BF16),
            pltpu.VMEM((ROWS_O, 128), BF16),
            pltpu.SMEM((HEADS,), F32),
            pltpu.VMEM((48, 128), F32),
            pltpu.VMEM((2, 16, 128), BF16),
            pltpu.VMEM((16, 16, 128), BF16),
            pltpu.VMEM((16, 16, 128), BF16),
            pltpu.VMEM((2, NX, NG, 16 * SLOTS, 128), BF16),
            pltpu.VMEM((2, NX, NG, 16 * ROWS_O, 128), BF16),
            pltpu.VMEM((2, 16, D), BF16),
            pltpu.VMEM((NZ, 16, HALF), BF16),
            pltpu.VMEM((NY, 16, HALF), BF16),
            pltpu.VMEM((NX, 16, HALF), BF16),
            pltpu.VMEM((464, D), BF16),
            pltpu.VMEM((D, D), BF16),
            pltpu.VMEM((16 * SLOTS, 16 * 16), BF16),
            pltpu.VMEM((11 * 128, 144), BF16),
            pltpu.VMEM((2, 144, HALF), BF16),
            pltpu.VMEM((2, 384, HALF), BF16),
            pltpu.VMEM((2, 384, HALF), BF16),
            pltpu.VMEM((2, 11 * 128, HALF), BF16),
            pltpu.VMEM((2, HALF, 128), BF16),
            pltpu.VMEM((HALF, 128), BF16),
            pltpu.SemaphoreType.DMA((COPIES,)),
            pltpu.SemaphoreType.DMA((COPIES,)),
            pltpu.SemaphoreType.DMA((4,)),
        ],
        compiler_params=pltpu.CompilerParams(
            collective_id=0, has_side_effects=True, vmem_limit_bytes=VMEM_BYTES
        ),
        name="layer",
    )(features, qkv_flat, out_flat, level_slope)


def solution(mesh):
    in_specs = (P("tm", None), P("tm", None), P("tm", None), P())
    return jax.shard_map(
        shards, mesh=mesh, in_specs=in_specs, out_specs=P("tm", None), check_vma=False
    )
```

```python
import math

import jax
import jax.numpy as jnp
from jax import lax
from jax.experimental import pallas as pl
from jax.experimental.pallas import tpu as pltpu
from jax.sharding import PartitionSpec as P

D = 768
HEADS = 12
HEAD_DIM = 64
BLOCK = 16
TOK = 128
NX, NY, NZ = 4, 8, 8
NG = 4
ROWS_Q, ROWS_O = 27, 9
SLOTS = 15
CUT_Q, CUT_O = 128, 80
HALF = D // 2
VMEM_BYTES = 60 * 2**20
LOG_TWO = math.log(2.0)
F32, BF16, I32 = jnp.float32, jnp.bfloat16, jnp.int32
MESH = pl.DeviceIdType.MESH


def iota(shape, dim):
    return lax.broadcasted_iota(I32, shape, dim)


def pick(condition, value=1.0):
    return jnp.where(condition, value, 0.0).astype(BF16)


def mm(a, b):
    return jnp.dot(a, b, preferred_element_type=F32)


def mm_nt(a, b):
    return lax.dot_general(a, b, (((1,), (1,)), ((), ())), preferred_element_type=F32)


def third(value):
    return lax.shift_right_logical(value * 171, 9)


def line_rows(place):
    row, col = iota((64, 128), 0), iota((64, 128), 1)
    r = row & 15
    first = pick((row < 16) & (col == 16 * (place ^ 1) + r))
    second = pick((row >= 16) & (row < 32) & ((col >> 1) == 16 * ((place >> 1) ^ 1) + r), 0.5)
    fourth = pick((row >= 32) & (row < 48) & ((col >> 2) == 16 * ((place >> 2) ^ 1) + r), 0.25)
    whole = pick((row >= 48) & ((col >> 3) == r), 0.125)
    return first + second + fourth + whole


def body(
    x_hbm, qkv_hbm, out_hbm, slope_hbm, o_ref,
    tokens_ref, qkv_ref, out_ref, slope_ref, stage, message, gather_q, gather_o, w_q, w_o,
    feat3, feat4, feat7, feat10,
    rows, order, perm, expand, q_all, k_all, v_all, q_exp, attended, away,
    send, recv, local,
):
    me = lax.axis_index("tm")
    x, y, z, c = me // 128, (me // 16) % 8, (me // 2) % 8, me % 2
    yq, yr, zq, zr = y // 4, y % 4, z // 4, z % 4

    loads = [
        pltpu.make_async_copy(x_hbm, tokens_ref, local.at[0]),
        pltpu.make_async_copy(qkv_hbm, qkv_ref, local.at[1]),
        pltpu.make_async_copy(out_hbm, out_ref, local.at[2]),
        pltpu.make_async_copy(slope_hbm, slope_ref, local.at[3]),
    ]
    for load in loads:
        load.start()

    def at(px, py, pz, pc):
        return ((px * NY + py) * NZ + pz) * 2 + pc

    sibling = at(x, y, z, 1 - c)
    steps = [(2, 2), (2, 1), (1, 2), (2, 3), (3, 2), (1, 1), (1, 3), (3, 1), (3, 3)]
    steps += [(0, 2), (2, 0), (0, 1), (1, 0), (0, 3), (3, 0)]
    square = [at(x, yq * 4 + (yr + j) % 4, zq * 4 + (zr + k) % 4, c) for j, k in steps]
    z_line = [at(x, y, (z + j) % 8, c) for j in (4, 3, 5, 2, 6, 1, 7)]
    y_line = [at(x, (y + j) % 8, z, c) for j in (4, 3, 5, 2, 6, 1, 7)]
    z_rest = [at(x, y, (1 - zq) * 4 + (zr + j) % 4, c) for j in range(4)]
    y_rest = [at(x, (1 - yq) * 4 + (yr + j) % 4, z, c) for j in range(4)]
    x_line = [at((x + j) % 4, y, z, c) for j in (2, 1, 3)]
    opposite, right, left = x_line
    z_mate = at(x, y, (z + 4 * (zr // 2) + 6) % 8, c)
    y_mate = at(x, (y + 4 * (yr // 2) + 6) % 8, z, c)

    barrier = pltpu.get_barrier_semaphore()
    greet = square + z_rest + y_rest + x_line + [sibling]
    for other in greet:
        pl.semaphore_signal(barrier, inc=1, device_id=(other,), device_id_type=MESH)

    sent = []

    def copy(ref, device, target=None):
        slot = len(sent)
        made = pltpu.make_async_remote_copy(
            src_ref=ref, dst_ref=ref if target is None else target, send_sem=send.at[slot], recv_sem=recv.at[slot],
            device_id=(device,), device_id_type=MESH,
        )
        made.start()
        sent.append(made)
        return made

    loads[1].wait()
    spot = yr * 4 + zr
    heads = z % 2
    partner = at(x, y, z + 1 - 2 * heads, c)
    stage[...] = jnp.zeros((48, 128), F32)
    stage[0:ROWS_Q, :] = qkv_ref[...].astype(F32)
    row, col = iota((32, 32), 0), iota((32, 32), 1)
    half, slot = row >> 4, row & 15
    s = third(slot)
    j = slot - 3 * s
    whole = 9 * c + 6 * s + 3 * half + j
    shared = jnp.where(slot < 12, 18 - 15 * c + 3 * half + j, 24 - 24 * c + j)
    source = jnp.where(slot < 9, whole, shared)
    wanted = (slot < 12) | ((slot < SLOTS) & (half == c))
    message[...] = mm(pick(wanted & (col == source)), stage[0:32, :].astype(BF16)).astype(BF16).reshape(2, 16, 128)
    gather_q[spot] = message[heads]

    pl.semaphore_wait(barrier, len(greet))

    first = [
        copy(message.at[(heads + k) % 2], other, gather_q.at[spot])
        for (j, k), other in zip(steps, square)
    ]

    for load in (loads[0], loads[2], loads[3]):
        load.wait()
    stage[32 : 32 + ROWS_O, :] = out_ref[...].astype(F32)
    gather_o[spot] = stage[32:48, :].astype(BF16)

    col = iota((1, D), 1)
    part = third(col >> 4)
    rest = col - 48 * part
    natural = (part >> 2) * 192 + ((part >> 1) & 1) * 96 + (part & 1) * 12
    natural = natural + ((rest >> 2) & 3) * 24 + (rest & 3) * 3 + (rest >> 4)
    order[...] = pick(iota((D, D), 0) == natural)
    tokens = mm(tokens_ref[...], order[...]).astype(BF16)
    rows[0:128, :] = tokens
    row, col = iota((16, 128), 0), iota((16, 128), 1)
    feat3[c] = mm(pick((col >> 3) == row, 0.125), tokens).astype(BF16)
    b = copy(feat3.at[c], sibling)
    row, col = iota((16 * SLOTS, 16 * 16), 0), iota((16 * SLOTS, 16 * 16), 1)
    perm[...] = pick(col == (row & 15) * 16 + (row >> 4))
    for level in range(1, 12):
        row, col = iota((128, 144), 0), iota((128, 144), 1)
        if level < 8:
            hit = (col < 128) & ((col >> level) == (row >> level))
            expand[pl.ds((level - 1) * 128, 128), :] = pick(hit, 0.125 / (1 << level))
        else:
            expand[pl.ds((level - 1) * 128, 128), :] = pick(col == 128 + level - 8, 0.125)

    b.wait_recv()
    mine = pl.ds(pl.multiple_of(c * HALF, 128), HALF)
    row, col = iota((16, 32), 0), iota((16, 32), 1)
    feat4[z] = mm(pick((col >> 1) == row, 0.5), feat3[:, :, mine].reshape(32, HALF)).astype(BF16)
    line = [copy(feat4.at[z], other) for other in z_line]
    second = [copy(gather_o.at[spot], other) for other in square]
    rows[432:448, :] = feat3[1 - c]
    pair3 = copy(feat3.at[1 - c], partner, rows.at[pl.ds(448, 16)])

    for made in first:
        made.wait_recv()
    own = 2 * yq + zq
    w_q[c, x, own] = mm(perm[...], gather_q[...].reshape(16 * 16, 128)).astype(BF16)
    over_z, over_y, far = 2 * yq + 1 - zq, 2 - 2 * yq + zq, 3 - own

    def got(made):
        for one in made:
            one.wait_recv()

    def along(ref):
        return [copy(ref.at[c, x, own], z_mate), copy(ref.at[c, x, own], y_mate)]

    def corner(ref, cut, size):
        return [
            copy(ref.at[c, x, over_z, pl.ds(0, cut)], y_mate),
            copy(ref.at[c, x, over_y, pl.ds(cut, size - cut)], z_mate),
        ]

    def along_x(ref, group, others):
        return [copy(ref.at[c, x, group], other) for other in others]

    def across(ref, px, group):
        return copy(ref.at[c, px, group], sibling)

    yz_q = along(w_q)
    x_q = [along_x(w_q, own, (opposite, right, left))]

    got(line)
    z_rows = feat4[...].reshape(128, HALF)
    found = mm(line_rows(z), z_rows).astype(BF16)
    rows[400:416, mine] = found[0:16]
    rows[416:432, mine] = feat4[z]
    rows[288:320, mine] = found[16:48]
    feat7[y] = found[48:]
    line = [copy(feat7.at[y], other) for other in y_line]
    row, col = iota((32, 128), 0), iota((32, 128), 1)
    chip = jnp.where(row < 16, z, z ^ 1)
    row = row & 15
    means = (
        pick((row == 0) & ((col >> 4) == chip), 1 / 16)
        + pick((row == 1) & ((col >> 5) == (z >> 1)), 1 / 32)
        + pick((row == 2) & ((col >> 6) == (z >> 2)), 1 / 64)
        + pick(row == 3, 1 / 128)
    )
    rows[256:288, mine] = mm(means, z_rows).astype(BF16)

    yz_q[0].wait_recv()
    yz_q[1].wait_recv()
    corner_q = corner(w_q, CUT_Q, 16 * SLOTS)
    pair_tokens = copy(rows.at[pl.ds(0, 128)], partner, rows.at[pl.ds(128, 128)])
    x_q.append(along_x(w_q, over_z, (opposite, right, left)))
    x_q.append(along_x(w_q, over_y, (opposite, right, left)))
    got(x_q[0])
    over = [across(w_q, (x + j) % 4, own) for j in (1, 2, 3)]
    got(second)
    w_o[c, x, own] = mm(perm[0 : 16 * ROWS_O, :], gather_o[...].reshape(16 * 16, 128)).astype(BF16)

    got(line)
    found = mm(line_rows(y), feat7[...].reshape(128, HALF)).astype(BF16)
    rows[320:368, mine] = found[:48]
    feat10[x] = found[48:]
    line = [copy(feat10.at[x], other) for other in x_line]

    got(corner_q)
    x_q.append(along_x(w_q, far, (opposite, right, left)))
    over.append(copy(w_q.at[c, x], sibling))
    yz_o = along(w_o)
    for n, group in ((1, over_z), (2, over_y)):
        got(x_q[n])
        over += [across(w_q, (x + j) % 4, group) for j in (1, 2, 3)]

    got(line)
    row, col = iota((32, 64), 0), iota((32, 64), 1)
    sides = pick((row < 16) & (col == 16 * (x ^ 1) + row)) + pick(
        (row >= 16) & ((col >> 1) == 16 * ((x >> 1) ^ 1) + row - 16), 0.5
    )
    rows[368:400, mine] = mm(sides, feat10[...].reshape(64, HALF)).astype(BF16)
    coarse = copy(rows.at[pl.ds(256, 176), mine], sibling)

    got(yz_o)
    corner_o = corner(w_o, CUT_O, 16 * ROWS_O)
    x_q[3][1].wait_recv()
    over.append(across(w_q, (x + 3) % 4, far))
    x_q[3][2].wait_recv()
    over.append(across(w_q, (x + 1) % 4, far))
    x_q[3][0].wait_recv()
    over.append(across(w_q, (x + 2) % 4, far))
    got(corner_o)
    x_o = [copy(w_o.at[c, x], other) for other in x_line]
    coarse.wait_recv()
    pair3.wait_recv()
    pair_tokens.wait_recv()
    got(over)
    over = [copy(w_o.at[c, x], sibling)]

    def tiles(sources):
        parts = []
        for px in range(NX):
            for group in range(NG):
                for ref, owner, place in sources:
                    parts.append(ref[owner, px, group, place * 16 : place * 16 + 16, :])
        return jnp.concatenate(parts, axis=0)

    def weight_q(s, j):
        second = ((0, 9 + j), (heads, 12 + j), (1, 9 + j))[s]
        return tiles([(w_q, 0, 3 * s + j), (w_q, *second), (w_q, 1, 3 * s + j)])

    def weight_o(n):
        second = (0, 6 + n) if n < 3 else (1, n - 3)
        return tiles([(w_o, 0, n), (w_o, *second), (w_o, 1, 3 + n)])

    row, col = iota((96, 128), 0), iota((96, 128), 1)
    pool = pick((row < 64) & ((col >> 1) == row), 0.5) + pick(
        (row >= 64) & ((col >> 2) == row - 64), 0.25
    )
    made = mm(rows[0:288, :], jnp.concatenate([weight_q(0, j) for j in range(3)], axis=1)).astype(BF16)
    for seg in range(2):
        q_all[seg, 0:128, :] = made[128 * seg : 128 * seg + 128]
        q_all[seg, 128:144, :] = made[256 + 16 * seg : 272 + 16 * seg]
        q_exp[seg] = mm(expand[...], q_all[seg]).astype(BF16)
    for kind, target in ((1, k_all), (2, v_all)):
        made = mm(rows[...], jnp.concatenate([weight_q(kind, j) for j in range(3)], axis=1)).astype(BF16)
        for seg in range(2):
            base = made[128 * seg : 128 * seg + 128]
            target[seg, 0:128, :] = base
            target[seg, 128:224, :] = mm(pool, base).astype(BF16)
            target[seg, 224:336, :] = made[288:400]
            target[seg, 336:352, :] = made[400 + 16 * seg : 416 + 16 * seg]
            target[seg, 352:368, :] = made[432 + 16 * seg : 448 + 16 * seg]
            target[seg, 368:384, :] = jnp.zeros((16, HALF), BF16)

    eye = pick(iota((128, 128), 0) == iota((128, 128), 1))
    lane = iota((128, 128), 1)
    key = iota((128, 128), 0)
    seen0 = (key >> 5) == (lane >> 5)
    seen1 = (key[:64] >> 4) == ((lane[:64] >> 5) ^ 1)
    seen2 = (key[:32] >> 4) == ((lane[:32] >> 6) ^ 1)
    spans = [(0, 0, 128), (1, 128, 192), (2, 192, 224)]
    spans += [(n, 144 + 16 * n, 160 + 16 * n) for n in range(5, 12)] + [(4, 336, 352), (3, 352, 368)]
    back = []
    for seg, pair in [(1, 0), (1, 1), (1, 2), (0, 0), (0, 1), (0, 2)]:
        if (seg, pair) == (0, 1):
            got(x_o)
            over += [copy(w_o.at[c, (x + j) % 4], sibling) for j in (1, 2, 3)]
        lanes = slice(pair * 128, (pair + 1) * 128)
        keys = k_all[seg, :, lanes]
        head_lane = iota((384, 128), 1)
        keys0 = jnp.where(head_lane < 64, keys, jnp.zeros_like(keys))
        keys1 = jnp.where(head_lane < 64, jnp.zeros_like(keys), keys)
        values = mm_nt(eye, v_all[seg, :, lanes]).astype(BF16)
        scores = [[], []]
        for level, low, high in spans:
            if level == 0:
                q = q_all[seg, 0:128, lanes] * jnp.asarray(0.125, BF16)
            else:
                q = q_exp[seg, pl.ds((level - 1) * 128, 128), lanes]
            both = mm_nt(jnp.concatenate([keys0[low:high], keys1[low:high]], axis=0), q)
            for side in range(2):
                part = both[side * (high - low) : (side + 1) * (high - low)]
                if level:
                    part = part + level * LOG_TWO * (1.0 - slope_ref[6 * heads + 2 * pair + side])
                if level < 3:
                    part = jnp.where((seen0, seen1, seen2)[level], part, -jnp.inf)
                scores[side].append(part)
        for side in range(2):
            flat = jnp.concatenate(scores[side], axis=0)
            top = jnp.max(flat, axis=0, keepdims=True)
            powers = jnp.exp(flat - top)
            total = jnp.sum(powers, axis=0, keepdims=True)
            powers = jnp.concatenate([powers, jnp.zeros((16, 128), F32)], axis=0).astype(BF16)
            part = mm(values[side * 64 : (side + 1) * 64], powers)
            part = (part / total).astype(BF16)
            if seg:
                away[pl.ds(pair * 128 + side * 64, 64), :] = part
            else:
                attended[heads, pl.ds(pair * 128 + side * 64, 64), :] = part
        if seg:
            piece = pl.ds(pair * 128, 128)
            back.append(copy(away.at[piece], partner, attended.at[heads, piece]))
    got(back)
    ready = mm(mm_nt(eye, attended[...].reshape(D, 128)).astype(BF16), order[...]).astype(BF16)

    got(over)
    for pair in range(3):
        w = jnp.concatenate([weight_o(2 * pair), weight_o(2 * pair + 1)], axis=1)
        o_ref[:, pair * 256 : (pair + 1) * 256] = mm(ready, w).astype(BF16)

    for made in sent:
        made.wait_send()


COPIES = 128


def shards(features, qkv_flat, out_flat, level_slope):
    hbm = pl.BlockSpec(memory_space=pl.ANY)
    return pl.pallas_call(
        body,
        out_shape=jax.ShapeDtypeStruct((TOK, D), BF16),
        in_specs=[hbm] * 4,
        out_specs=pl.BlockSpec(memory_space=pltpu.VMEM),
        scratch_shapes=[
            pltpu.VMEM((TOK, D), BF16),
            pltpu.VMEM((ROWS_Q, 128), BF16),
            pltpu.VMEM((ROWS_O, 128), BF16),
            pltpu.SMEM((HEADS,), F32),
            pltpu.VMEM((48, 128), F32),
            pltpu.VMEM((2, 16, 128), BF16),
            pltpu.VMEM((16, 16, 128), BF16),
            pltpu.VMEM((16, 16, 128), BF16),
            pltpu.VMEM((2, NX, NG, 16 * SLOTS, 128), BF16),
            pltpu.VMEM((2, NX, NG, 16 * ROWS_O, 128), BF16),
            pltpu.VMEM((2, 16, D), BF16),
            pltpu.VMEM((NZ, 16, HALF), BF16),
            pltpu.VMEM((NY, 16, HALF), BF16),
            pltpu.VMEM((NX, 16, HALF), BF16),
            pltpu.VMEM((464, D), BF16),
            pltpu.VMEM((D, D), BF16),
            pltpu.VMEM((16 * SLOTS, 16 * 16), BF16),
            pltpu.VMEM((11 * 128, 144), BF16),
            pltpu.VMEM((2, 144, HALF), BF16),
            pltpu.VMEM((2, 384, HALF), BF16),
            pltpu.VMEM((2, 384, HALF), BF16),
            pltpu.VMEM((2, 11 * 128, HALF), BF16),
            pltpu.VMEM((2, HALF, 128), BF16),
            pltpu.VMEM((HALF, 128), BF16),
            pltpu.SemaphoreType.DMA((COPIES,)),
            pltpu.SemaphoreType.DMA((COPIES,)),
            pltpu.SemaphoreType.DMA((4,)),
        ],
        compiler_params=pltpu.CompilerParams(
            collective_id=0, has_side_effects=True, vmem_limit_bytes=VMEM_BYTES
        ),
        name="layer",
    )(features, qkv_flat, out_flat, level_slope)


def solution(mesh):
    in_specs = (P("tm", None), P("tm", None), P("tm", None), P())
    return jax.shard_map(
        shards, mesh=mesh, in_specs=in_specs, out_specs=P("tm", None), check_vma=False
    )
```

```python
import math

import jax
import jax.numpy as jnp
from jax import lax
from jax.experimental import pallas as pl
from jax.experimental.pallas import tpu as pltpu
from jax.sharding import PartitionSpec as P

D = 768
HEADS = 12
HEAD_DIM = 64
BLOCK = 16
TOK = 128
NX, NY, NZ = 4, 8, 8
NG = 4
ROWS_Q, ROWS_O = 27, 9
SLOTS = 15
CUT_Q, CUT_O = 128, 80
HALF = D // 2
VMEM_BYTES = 60 * 2**20
LOG_TWO = math.log(2.0)
F32, BF16, I32 = jnp.float32, jnp.bfloat16, jnp.int32
MESH = pl.DeviceIdType.MESH


def iota(shape, dim):
    return lax.broadcasted_iota(I32, shape, dim)


def pick(condition, value=1.0):
    return jnp.where(condition, value, 0.0).astype(BF16)


def mm(a, b):
    return jnp.dot(a, b, preferred_element_type=F32)


def mm_nt(a, b):
    return lax.dot_general(a, b, (((1,), (1,)), ((), ())), preferred_element_type=F32)


def third(value):
    return lax.shift_right_logical(value * 171, 9)


def line_rows(place):
    row, col = iota((64, 128), 0), iota((64, 128), 1)
    r = row & 15
    first = pick((row < 16) & (col == 16 * (place ^ 1) + r))
    second = pick((row >= 16) & (row < 32) & ((col >> 1) == 16 * ((place >> 1) ^ 1) + r), 0.5)
    fourth = pick((row >= 32) & (row < 48) & ((col >> 2) == 16 * ((place >> 2) ^ 1) + r), 0.25)
    whole = pick((row >= 48) & ((col >> 3) == r), 0.125)
    return first + second + fourth + whole


def body(
    x_hbm, qkv_hbm, out_hbm, slope_hbm, o_ref,
    tokens_ref, qkv_ref, out_ref, slope_ref, stage, message, gather_q, gather_o, w_q, w_o,
    feat3, feat4, feat7, feat10,
    rows, order, perm, expand, q_all, k_all, v_all, q_exp, attended, away,
    send, recv, local,
):
    me = lax.axis_index("tm")
    x, y, z, c = me // 128, (me // 16) % 8, (me // 2) % 8, me % 2
    yq, yr, zq, zr = y // 4, y % 4, z // 4, z % 4

    loads = [
        pltpu.make_async_copy(x_hbm, tokens_ref, local.at[0]),
        pltpu.make_async_copy(qkv_hbm, qkv_ref, local.at[1]),
        pltpu.make_async_copy(out_hbm, out_ref, local.at[2]),
        pltpu.make_async_copy(slope_hbm, slope_ref, local.at[3]),
    ]
    for load in loads:
        load.start()

    def at(px, py, pz, pc):
        return ((px * NY + py) * NZ + pz) * 2 + pc

    sibling = at(x, y, z, 1 - c)
    steps = [(j, k) for j in range(4) for k in range(4) if j or k]
    square = [at(x, yq * 4 + (yr + j) % 4, zq * 4 + (zr + k) % 4, c) for j, k in steps]
    z_line = [at(x, y, (z + j) % 8, c) for j in (4, 3, 5, 2, 6, 1, 7)]
    y_line = [at(x, (y + j) % 8, z, c) for j in (4, 3, 5, 2, 6, 1, 7)]
    z_rest = [at(x, y, (1 - zq) * 4 + (zr + j) % 4, c) for j in range(4)]
    y_rest = [at(x, (1 - yq) * 4 + (yr + j) % 4, z, c) for j in range(4)]
    x_line = [at((x + j) % 4, y, z, c) for j in (2, 1, 3)]
    opposite, right, left = x_line
    z_mate = at(x, y, (z + 4 * (zr // 2) + 6) % 8, c)
    y_mate = at(x, (y + 4 * (yr // 2) + 6) % 8, z, c)

    barrier = pltpu.get_barrier_semaphore()
    greet = square + z_rest + y_rest + x_line + [sibling]
    for other in greet:
        pl.semaphore_signal(barrier, inc=1, device_id=(other,), device_id_type=MESH)

    sent = []

    def copy(ref, device, target=None):
        slot = len(sent)
        made = pltpu.make_async_remote_copy(
            src_ref=ref, dst_ref=ref if target is None else target, send_sem=send.at[slot], recv_sem=recv.at[slot],
            device_id=(device,), device_id_type=MESH,
        )
        made.start()
        sent.append(made)
        return made

    loads[1].wait()
    spot = yr * 4 + zr
    heads = z % 2
    partner = at(x, y, z + 1 - 2 * heads, c)
    stage[...] = jnp.zeros((48, 128), F32)
    stage[0:ROWS_Q, :] = qkv_ref[...].astype(F32)
    row, col = iota((32, 32), 0), iota((32, 32), 1)
    half, slot = row >> 4, row & 15
    s = third(slot)
    j = slot - 3 * s
    whole = 9 * c + 6 * s + 3 * half + j
    shared = jnp.where(slot < 12, 18 - 15 * c + 3 * half + j, 24 - 24 * c + j)
    source = jnp.where(slot < 9, whole, shared)
    wanted = (slot < 12) | ((slot < SLOTS) & (half == c))
    message[...] = mm(pick(wanted & (col == source)), stage[0:32, :].astype(BF16)).astype(BF16).reshape(2, 16, 128)
    gather_q[spot] = message[heads]

    pl.semaphore_wait(barrier, len(greet))

    first = [
        copy(message.at[(heads + k) % 2], other, gather_q.at[spot])
        for (j, k), other in zip(steps, square)
    ]

    for load in (loads[0], loads[2], loads[3]):
        load.wait()
    stage[32 : 32 + ROWS_O, :] = out_ref[...].astype(F32)
    gather_o[spot] = stage[32:48, :].astype(BF16)

    col = iota((1, D), 1)
    part = third(col >> 4)
    rest = col - 48 * part
    natural = (part >> 2) * 192 + ((part >> 1) & 1) * 96 + (part & 1) * 12
    natural = natural + ((rest >> 2) & 3) * 24 + (rest & 3) * 3 + (rest >> 4)
    order[...] = pick(iota((D, D), 0) == natural)
    tokens = mm(tokens_ref[...], order[...]).astype(BF16)
    rows[0:128, :] = tokens
    row, col = iota((16, 128), 0), iota((16, 128), 1)
    feat3[c] = mm(pick((col >> 3) == row, 0.125), tokens).astype(BF16)
    b = copy(feat3.at[c], sibling)
    row, col = iota((16 * SLOTS, 16 * 16), 0), iota((16 * SLOTS, 16 * 16), 1)
    perm[...] = pick(col == (row & 15) * 16 + (row >> 4))
    for level in range(1, 12):
        row, col = iota((128, 144), 0), iota((128, 144), 1)
        if level < 8:
            hit = (col < 128) & ((col >> level) == (row >> level))
            expand[pl.ds((level - 1) * 128, 128), :] = pick(hit, 0.125 / (1 << level))
        else:
            expand[pl.ds((level - 1) * 128, 128), :] = pick(col == 128 + level - 8, 0.125)

    b.wait_recv()
    mine = pl.ds(pl.multiple_of(c * HALF, 128), HALF)
    row, col = iota((16, 32), 0), iota((16, 32), 1)
    feat4[z] = mm(pick((col >> 1) == row, 0.5), feat3[:, :, mine].reshape(32, HALF)).astype(BF16)
    line = [copy(feat4.at[z], other) for other in z_line]
    second = [copy(gather_o.at[spot], other) for other in square]
    rows[432:448, :] = feat3[1 - c]
    pair3 = copy(feat3.at[1 - c], partner, rows.at[pl.ds(448, 16)])

    for made in first:
        made.wait_recv()
    own = 2 * yq + zq
    w_q[c, x, own] = mm(perm[...], gather_q[...].reshape(16 * 16, 128)).astype(BF16)
    over_z, over_y, far = 2 * yq + 1 - zq, 2 - 2 * yq + zq, 3 - own

    def got(made):
        for one in made:
            one.wait_recv()

    def along(ref):
        return [copy(ref.at[c, x, own], z_mate), copy(ref.at[c, x, own], y_mate)]

    def corner(ref, cut, size):
        return [
            copy(ref.at[c, x, over_z, pl.ds(0, cut)], y_mate),
            copy(ref.at[c, x, over_y, pl.ds(cut, size - cut)], z_mate),
        ]

    def along_x(ref, group, others):
        return [copy(ref.at[c, x, group], other) for other in others]

    def across(ref, px, group):
        return copy(ref.at[c, px, group], sibling)

    yz_q = along(w_q)
    x_q = [along_x(w_q, own, (opposite, right, left))]

    got(line)
    z_rows = feat4[...].reshape(128, HALF)
    found = mm(line_rows(z), z_rows).astype(BF16)
    rows[400:416, mine] = found[0:16]
    rows[416:432, mine] = feat4[z]
    rows[288:320, mine] = found[16:48]
    feat7[y] = found[48:]
    line = [copy(feat7.at[y], other) for other in y_line]
    row, col = iota((32, 128), 0), iota((32, 128), 1)
    chip = jnp.where(row < 16, z, z ^ 1)
    row = row & 15
    means = (
        pick((row == 0) & ((col >> 4) == chip), 1 / 16)
        + pick((row == 1) & ((col >> 5) == (z >> 1)), 1 / 32)
        + pick((row == 2) & ((col >> 6) == (z >> 2)), 1 / 64)
        + pick(row == 3, 1 / 128)
    )
    rows[256:288, mine] = mm(means, z_rows).astype(BF16)

    yz_q[0].wait_recv()
    yz_q[1].wait_recv()
    corner_q = corner(w_q, CUT_Q, 16 * SLOTS)
    pair_tokens = copy(rows.at[pl.ds(0, 128)], partner, rows.at[pl.ds(128, 128)])
    x_q.append(along_x(w_q, over_z, (opposite, right, left)))
    x_q.append(along_x(w_q, over_y, (opposite, right, left)))
    got(x_q[0])
    over = [across(w_q, (x + j) % 4, own) for j in (1, 2, 3)]
    got(second)
    w_o[c, x, own] = mm(perm[0 : 16 * ROWS_O, :], gather_o[...].reshape(16 * 16, 128)).astype(BF16)

    got(line)
    found = mm(line_rows(y), feat7[...].reshape(128, HALF)).astype(BF16)
    rows[320:368, mine] = found[:48]
    feat10[x] = found[48:]
    line = [copy(feat10.at[x], other) for other in x_line]

    got(corner_q)
    x_q.append(along_x(w_q, far, (opposite, right, left)))
    over.append(copy(w_q.at[c, x], sibling))
    yz_o = along(w_o)
    for n, group in ((1, over_z), (2, over_y)):
        got(x_q[n])
        over += [across(w_q, (x + j) % 4, group) for j in (1, 2, 3)]

    got(line)
    row, col = iota((32, 64), 0), iota((32, 64), 1)
    sides = pick((row < 16) & (col == 16 * (x ^ 1) + row)) + pick(
        (row >= 16) & ((col >> 1) == 16 * ((x >> 1) ^ 1) + row - 16), 0.5
    )
    rows[368:400, mine] = mm(sides, feat10[...].reshape(64, HALF)).astype(BF16)
    coarse = copy(rows.at[pl.ds(256, 176), mine], sibling)

    got(yz_o)
    corner_o = corner(w_o, CUT_O, 16 * ROWS_O)
    x_q[3][1].wait_recv()
    over.append(across(w_q, (x + 3) % 4, far))
    x_q[3][2].wait_recv()
    over.append(across(w_q, (x + 1) % 4, far))
    x_q[3][0].wait_recv()
    over.append(across(w_q, (x + 2) % 4, far))
    got(corner_o)
    x_o = [copy(w_o.at[c, x], other) for other in x_line]
    coarse.wait_recv()
    pair3.wait_recv()
    pair_tokens.wait_recv()
    got(over)
    over = [copy(w_o.at[c, x], sibling)]

    def tiles(sources):
        parts = []
        for px in range(NX):
            for group in range(NG):
                for ref, owner, place in sources:
                    parts.append(ref[owner, px, group, place * 16 : place * 16 + 16, :])
        return jnp.concatenate(parts, axis=0)

    def weight_q(s, j):
        second = ((0, 9 + j), (heads, 12 + j), (1, 9 + j))[s]
        return tiles([(w_q, 0, 3 * s + j), (w_q, *second), (w_q, 1, 3 * s + j)])

    def weight_o(n):
        second = (0, 6 + n) if n < 3 else (1, n - 3)
        return tiles([(w_o, 0, n), (w_o, *second), (w_o, 1, 3 + n)])

    row, col = iota((96, 128), 0), iota((96, 128), 1)
    pool = pick((row < 64) & ((col >> 1) == row), 0.5) + pick(
        (row >= 64) & ((col >> 2) == row - 64), 0.25
    )
    made = mm(rows[0:288, :], jnp.concatenate([weight_q(0, j) for j in range(3)], axis=1)).astype(BF16)
    for seg in range(2):
        q_all[seg, 0:128, :] = made[128 * seg : 128 * seg + 128]
        q_all[seg, 128:144, :] = made[256 + 16 * seg : 272 + 16 * seg]
        q_exp[seg] = mm(expand[...], q_all[seg]).astype(BF16)
    for kind, target in ((1, k_all), (2, v_all)):
        made = mm(rows[...], jnp.concatenate([weight_q(kind, j) for j in range(3)], axis=1)).astype(BF16)
        for seg in range(2):
            base = made[128 * seg : 128 * seg + 128]
            target[seg, 0:128, :] = base
            target[seg, 128:224, :] = mm(pool, base).astype(BF16)
            target[seg, 224:336, :] = made[288:400]
            target[seg, 336:352, :] = made[400 + 16 * seg : 416 + 16 * seg]
            target[seg, 352:368, :] = made[432 + 16 * seg : 448 + 16 * seg]
            target[seg, 368:384, :] = jnp.zeros((16, HALF), BF16)

    eye = pick(iota((128, 128), 0) == iota((128, 128), 1))
    lane = iota((128, 128), 1)
    key = iota((128, 128), 0)
    seen0 = (key >> 5) == (lane >> 5)
    seen1 = (key[:64] >> 4) == ((lane[:64] >> 5) ^ 1)
    seen2 = (key[:32] >> 4) == ((lane[:32] >> 6) ^ 1)
    spans = [(0, 0, 128), (1, 128, 192), (2, 192, 224)]
    spans += [(n, 144 + 16 * n, 160 + 16 * n) for n in range(5, 12)] + [(4, 336, 352), (3, 352, 368)]
    back = []
    for seg, pair in [(1, 0), (1, 1), (1, 2), (0, 0), (0, 1), (0, 2)]:
        if (seg, pair) == (0, 1):
            got(x_o)
            over += [copy(w_o.at[c, (x + j) % 4], sibling) for j in (1, 2, 3)]
        lanes = slice(pair * 128, (pair + 1) * 128)
        keys = k_all[seg, :, lanes]
        head_lane = iota((384, 128), 1)
        keys0 = jnp.where(head_lane < 64, keys, jnp.zeros_like(keys))
        keys1 = jnp.where(head_lane < 64, jnp.zeros_like(keys), keys)
        values = mm_nt(eye, v_all[seg, :, lanes]).astype(BF16)
        scores = [[], []]
        for level, low, high in spans:
            if level == 0:
                q = q_all[seg, 0:128, lanes] * jnp.asarray(0.125, BF16)
            else:
                q = q_exp[seg, pl.ds((level - 1) * 128, 128), lanes]
            both = mm_nt(jnp.concatenate([keys0[low:high], keys1[low:high]], axis=0), q)
            for side in range(2):
                part = both[side * (high - low) : (side + 1) * (high - low)]
                if level:
                    part = part + level * LOG_TWO * (1.0 - slope_ref[6 * heads + 2 * pair + side])
                if level < 3:
                    part = jnp.where((seen0, seen1, seen2)[level], part, -jnp.inf)
                scores[side].append(part)
        for side in range(2):
            flat = jnp.concatenate(scores[side], axis=0)
            top = jnp.max(flat, axis=0, keepdims=True)
            powers = jnp.exp(flat - top)
            total = jnp.sum(powers, axis=0, keepdims=True)
            powers = jnp.concatenate([powers, jnp.zeros((16, 128), F32)], axis=0).astype(BF16)
            part = mm(values[side * 64 : (side + 1) * 64], powers)
            part = (part / total).astype(BF16)
            if seg:
                away[pl.ds(pair * 128 + side * 64, 64), :] = part
            else:
                attended[heads, pl.ds(pair * 128 + side * 64, 64), :] = part
        if seg:
            piece = pl.ds(pair * 128, 128)
            back.append(copy(away.at[piece], partner, attended.at[heads, piece]))
    got(back)
    ready = mm(mm_nt(eye, attended[...].reshape(D, 128)).astype(BF16), order[...]).astype(BF16)

    got(over)
    for pair in range(3):
        w = jnp.concatenate([weight_o(2 * pair), weight_o(2 * pair + 1)], axis=1)
        o_ref[:, pair * 256 : (pair + 1) * 256] = mm(ready, w).astype(BF16)

    for made in sent:
        made.wait_send()


COPIES = 128


def shards(features, qkv_flat, out_flat, level_slope):
    hbm = pl.BlockSpec(memory_space=pl.ANY)
    return pl.pallas_call(
        body,
        out_shape=jax.ShapeDtypeStruct((TOK, D), BF16),
        in_specs=[hbm] * 4,
        out_specs=pl.BlockSpec(memory_space=pltpu.VMEM),
        scratch_shapes=[
            pltpu.VMEM((TOK, D), BF16),
            pltpu.VMEM((ROWS_Q, 128), BF16),
            pltpu.VMEM((ROWS_O, 128), BF16),
            pltpu.SMEM((HEADS,), F32),
            pltpu.VMEM((48, 128), F32),
            pltpu.VMEM((2, 16, 128), BF16),
            pltpu.VMEM((16, 16, 128), BF16),
            pltpu.VMEM((16, 16, 128), BF16),
            pltpu.VMEM((2, NX, NG, 16 * SLOTS, 128), BF16),
            pltpu.VMEM((2, NX, NG, 16 * ROWS_O, 128), BF16),
            pltpu.VMEM((2, 16, D), BF16),
            pltpu.VMEM((NZ, 16, HALF), BF16),
            pltpu.VMEM((NY, 16, HALF), BF16),
            pltpu.VMEM((NX, 16, HALF), BF16),
            pltpu.VMEM((464, D), BF16),
            pltpu.VMEM((D, D), BF16),
            pltpu.VMEM((16 * SLOTS, 16 * 16), BF16),
            pltpu.VMEM((11 * 128, 144), BF16),
            pltpu.VMEM((2, 144, HALF), BF16),
            pltpu.VMEM((2, 384, HALF), BF16),
            pltpu.VMEM((2, 384, HALF), BF16),
            pltpu.VMEM((2, 11 * 128, HALF), BF16),
            pltpu.VMEM((2, HALF, 128), BF16),
            pltpu.VMEM((HALF, 128), BF16),
            pltpu.SemaphoreType.DMA((COPIES,)),
            pltpu.SemaphoreType.DMA((COPIES,)),
            pltpu.SemaphoreType.DMA((4,)),
        ],
        compiler_params=pltpu.CompilerParams(
            collective_id=0, has_side_effects=True, vmem_limit_bytes=VMEM_BYTES
        ),
        name="layer",
    )(features, qkv_flat, out_flat, level_slope)


def solution(mesh):
    in_specs = (P("tm", None), P("tm", None), P("tm", None), P())
    return jax.shard_map(
        shards, mesh=mesh, in_specs=in_specs, out_specs=P("tm", None), check_vma=False
    )
```
